256 devices in a mesh: dp: 32 (over x, y, z_hi), tensor: 8 (over z_lo, core).
Axes of the slice: x: 4, y: 4, z: 8 (z_hi: 2, z_lo: 4; z = z_hi * 4 + z_lo), core: 2. Of those that a mesh axis runs over, the one named last changes fastest.
Arguments:
- tokens: bfloat16 [1024, 16384], P('dp', 'tensor'), may hold values from -6 to 6
- gate_weight: bfloat16 [16384, 28672], P('tensor', 'dp'), may hold values from -0.046875 to 0.046875
- up_weight: bfloat16 [16384, 28672], P('tensor', 'dp'), may hold values from -0.046875 to 0.046875
- down_weight: bfloat16 [28672, 16384], P('dp', 'tensor'), may hold values from -0.03125 to 0.03125
Outputs:
- mixed: bfloat16 [1024, 16384], P('dp', 'tensor')
The draws below stay inside these ranges and needn't reach their ends.
All inputs are finite; a program needn't handle non-finite values.
Results may differ from the reference program's by a relative error of at most 0.0049.
Values may be sent and summed in bfloat16 or wider, within the bound.
A program may use at most 128 MiB of HBM per device.

```python
import jax
import jax.numpy as jnp

D = 16384
FFW = 28672
TOKENS = 1024


def block_levels(key, dims, pieces, least, largest):
    def one(position, parts):
        draws = jax.random.uniform(jax.random.fold_in(jax.random.fold_in(key, 6), position), (parts,), jnp.float32, least / len(pieces), largest / len(pieces))
        return jnp.repeat(jnp.exp(draws), dims[position] // parts).reshape((-1,) + (1,) * (len(dims) - position - 1))

    factor_of = one(*pieces[0])
    for cut in pieces[1:]:
        factor_of = factor_of * one(*cut)
    return factor_of


def scatter_about(own_key, shape, width, reach, cuts=(), dtype=jnp.bfloat16):
    factor_of = block_levels(own_key, shape, cuts, -0.22, 0.18) if cuts else 1.0
    entries = jax.random.normal(own_key, shape, jnp.float32) * width * factor_of
    return jnp.minimum(jnp.maximum(entries, -reach), reach).astype(dtype)


def setup_inputs(seed: int = 0) -> dict:
    key_list = jax.random.split(jax.random.key(seed), 5)
    return {
        "tokens": scatter_about(key_list[0], (TOKENS, D), 1.0, 6.0, ((0, 32), (1, 8))),
        "gate_weight": scatter_about(key_list[1], (D, FFW), D ** -0.5, 0.046875, ((0, 8), (1, 32))),
        "up_weight": scatter_about(key_list[2], (D, FFW), D ** -0.5, 0.046875, ((0, 8), (1, 32))),
        "down_weight": scatter_about(key_list[3], (FFW, D), FFW ** -0.5, 0.03125, ((0, 32), (1, 8))),
    }


def reference(tokens, gate_weight, up_weight, down_weight):
    gate = jnp.dot(tokens, gate_weight, preferred_element_type=jnp.float32)
    up = jnp.dot(tokens, up_weight, preferred_element_type=jnp.float32)
    hidden = (jax.nn.silu(gate) * up).astype(jnp.bfloat16)
    return jnp.dot(hidden, down_weight, preferred_element_type=jnp.float32).astype(jnp.bfloat16)
```

```python
import jax
import jax.numpy as jnp
from jax import lax
from jax.experimental import pallas as pl
from jax.experimental.pallas import tpu as pltpu
from jax.sharding import PartitionSpec as P

F32, BF16 = jnp.float32, jnp.bfloat16
CHUNKS = 4
OWN, OTHER, HALF_OF = (0, 3), (1, 2), (0, 0, 1, 1)
SPLIT = ((0, 4), (4, 7))
WIDE = F32


class Sends:
    def __init__(self, send_sem, recv_sem):
        self.send_sem, self.recv_sem = send_sem, recv_sem
        self.ids, self.open = {}, []

    def copy(self, name, src, dst, device):
        number = self.ids.setdefault(name, len(self.ids))
        return pltpu.make_async_remote_copy(
            src_ref=src,
            dst_ref=dst,
            send_sem=self.send_sem.at[number],
            recv_sem=self.recv_sem.at[number],
            device_id=device,
            device_id_type=pl.DeviceIdType.MESH,
        )

    def start(self, name, src, dst, device, when=None):
        one = self.copy(name, src, dst, device)
        one.start()
        self.open.append((one, when))

    def arrived(self, name, dst, device):
        self.copy(name, dst, dst, device).wait_recv()

    def finish(self):
        for one, when in self.open:
            if when is None:
                one.wait_send()
            else:
                pl.when(when)(one.wait_send)


TRANSFERS = 192


def kernel(tokens, gate, up, down, out, tok, wgu, wd, part, pair, zs, zr, hid, mix, s1, r1, t1, r2, t2, z3, local_sem, send_sem, recv_sem):
    dp, tensor = lax.axis_index("dp"), lax.axis_index("tensor")
    x, y, zh = dp // 8, (dp // 2) % 4, dp % 2
    zl, core = tensor // 2, tensor % 2
    pos = jnp.where(core == 0, zl, 3 - zl)
    step = jnp.where(core == 0, 1, -1)

    def plane(dx, dy):
        return ((((x + dx + 4) % 4) * 4 + (y + dy + 4) % 4) * 2 + zh, tensor)

    across = ((x * 4 + y) * 2 + 1 - zh, tensor)
    mate = (dp, zl * 2 + 1 - core)
    ahead = (dp, (zl + step) * 2 + core)
    behind = (dp, (zl - step) * 2 + core)

    mine = [
        pltpu.make_async_copy(tokens.at[pl.ds(16 * h, 16)], tok.at[OWN[h], y, x], local_sem.at[h])
        for h in range(2)
    ]
    weights = []
    for n in range(7):
        for g, ref in enumerate((gate, up)):
            weights.append(
                pltpu.make_async_copy(
                    ref.at[:, pl.ds(128 * n, 128)],
                    wgu.at[:, pl.ds(256 * n + 128 * g, 128)],
                    local_sem.at[2 + 2 * n + g],
                )
            )
    weights.append(pltpu.make_async_copy(down, wd, local_sem.at[16]))
    for one in mine + weights:
        one.start()

    barrier = pltpu.get_barrier_semaphore()

    def greet(device):
        pl.semaphore_signal(barrier, inc=1, device_id=device, device_id_type=pl.DeviceIdType.MESH)

    for dx, dy in ((1, 0), (-1, 0), (2, 0), (0, 1), (0, -1), (0, 2)):
        greet(plane(dx, dy))
    greet(across)
    greet(mate)
    pl.when(pos < 3)(lambda: greet(ahead))
    pl.when(pos > 0)(lambda: greet(behind))
    pl.semaphore_wait(barrier, 8 + jnp.where(pos < 3, 1, 0) + jnp.where(pos > 0, 1, 0))

    net = Sends(send_sem, recv_sem)

    def light(s, d):
        return plane(d, 0) if s == 0 else plane(0, d)

    def heavy(s, d):
        return plane(0, d) if s == 0 else plane(d, 0)

    here = ((y, x), (x, y))

    def at(ref, k, s, a, b):
        cols = pl.ds(1024 * s, 1024)
        return ref.at[k, a, b, :, cols] if s == 0 else ref.at[k, b, a, :, cols]

    every, low, high = pl.ds(0, 4), pl.ds(0, 2), pl.ds(2, 2)

    def tokens_out(h):
        mine[h].wait()
        net.start(("z", h), tok.at[OWN[h], y, x], tok.at[OTHER[h], y, x], across)

    def tokens_light(k):
        if k in OTHER:
            h = HALF_OF[k]
            net.arrived(("z", h), tok.at[k, y, x], across)
        for s in range(2):
            a, b = here[s]
            block = at(tok, k, s, a, b)
            for i, d in enumerate((1, -1, 2)):
                net.start(("light", k, s, i), block, block, light(s, d))

    def tokens_heavy(k, s):
        a, b = here[s]
        for i, d in enumerate((1, -1, 2)):
            net.arrived(("light", k, s, i), at(tok, k, s, a, (b - d + 4) % 4), light(s, d))
        line = at(tok, k, s, a, every)
        for i, d in enumerate((1, -1)):
            net.start(("heavy", k, s, i), line, line, heavy(s, d))

    def tokens_forward(k, s):
        a, b = here[s]
        for i, (d, half) in enumerate(((1, low), (-1, high))):
            net.arrived(("heavy", k, s, i), at(tok, k, s, (a - d + 4) % 4, every), heavy(s, d))
            block = at(tok, k, s, (a - d + 4) % 4, half)
            net.start(("forward", k, s, i), block, block, heavy(s, d))

    def tokens_in(k):
        for s in range(2):
            a, b = here[s]
            for i, (d, half) in enumerate(((1, low), (-1, high))):
                net.arrived(("forward", k, s, i), at(tok, k, s, (a + 2) % 4, half), heavy(s, d))

    def columns(j):
        return pl.ds(256 * SPLIT[j][0], 256 * (SPLIT[j][1] - SPLIT[j][0]))

    def units(j):
        return pl.ds(128 * SPLIT[j][0], 128 * (SPLIT[j][1] - SPLIT[j][0]))

    def multiply(k, j):
        if k == 0:
            for one in weights[2 * SPLIT[j][0] : 2 * SPLIT[j][1]]:
                one.wait()

        @pl.loop(*SPLIT[j])
        def _(n):
            cols = pl.ds(pl.multiple_of(n * 256, 256), 256)
            value = jnp.dot(tok[k].reshape(256, 2048), wgu[:, cols], preferred_element_type=F32)
            part[k, :, :, cols] = value.reshape(2, 128, 256)

        net.start(("pair", k, j), part.at[k, 1 - core, :, columns(j)], pair.at[k, :, columns(j)], mate)

    def total(k, j, rows, more):
        cols = columns(j)
        value = part[k, core, rows, cols] + pair[k, rows, cols]
        if more:
            value = value + zr[k, rows, cols].astype(F32)
        return value

    def pass_on(k, j, more):
        @pl.loop(0, 8)
        def _(r):
            rows = pl.ds(pl.multiple_of(r * 16, 16), 16)
            zs[k, rows, columns(j)] = total(k, j, rows, more).astype(BF16)

        net.start(("line", k, j), zs.at[k, :, columns(j)], zr.at[k, :, columns(j)], ahead, pos < 3)

    def line_in(k, j):
        net.arrived(("line", k, j), zr.at[k, :, columns(j)], behind)

    def line(k, j, p):
        if p == 0:
            net.arrived(("pair", k, j), pair.at[k, :, columns(j)], mate)

        def go():
            if p:
                line_in(k, j)
            if p < 3:
                pass_on(k, j, p > 0)
            else:
                activate(k, j)

        kept = net.open[:]
        pl.when(pos == p)(go)
        net.open = kept

    def block_of(k, j):
        return hid.at[k, core, :, units(j)]

    def share(k, j):
        net.start(("share", k, j), block_of(k, j), block_of(k, j), mate)

    def hand_back(k, j):
        net.start(("back", k, j), block_of(k, j), block_of(k, j), behind)

    def activate(k, j):
        @pl.loop(0, 8)
        def _(r):
            rows = pl.ds(pl.multiple_of(r * 16, 16), 16)
            value = total(k, j, rows, True)
            for n in range(SPLIT[j][1] - SPLIT[j][0]):
                g, u = value[:, 256 * n : 256 * n + 128], value[:, 256 * n + 128 : 256 * n + 256]
                unit = 128 * (SPLIT[j][0] + n)
                hid[k, core, rows, unit : unit + 128] = (g / (1.0 + jnp.exp(-g)) * u).astype(BF16)

        hand_back(k, j)
        share(k, j)

    def back(k, j, p):
        def go():
            net.arrived(("back", k, j), block_of(k, j), ahead)
            if p > 0:
                hand_back(k, j)
            share(k, j)

        kept = net.open[:]
        pl.when(pos == p)(go)
        net.open = kept

    def project(k, s):
        if s == 0:
            if k == 0:
                weights[14].wait()
            for j in range(2):
                net.arrived(("share", k, j), hid.at[k, 1 - core, :, units(j)], mate)

        @pl.loop(4 * s, 4 * s + 4)
        def _(n):
            cols = pl.ds(pl.multiple_of(n * 256, 256), 256)
            value = jnp.dot(hid[k].reshape(256, 896), wd[:, cols], preferred_element_type=F32)
            mix[k, :, :, :, cols] = value.reshape(4, 4, 16, 256)

        a, b = here[s]
        for m, (to, d, half) in enumerate(((2, 1, low), (2, -1, high), (1, 1, high), (-1, -1, low))):
            s1[k, s, m] = at(mix, k, s, (a + to + 4) % 4, half)[...].astype(BF16)
            net.start(("first", k, s, m), s1.at[k, s, m], r1.at[k, s, m], heavy(s, d))

    def scatter_sum(k, s):
        a, b = here[s]
        for m, (d, half) in enumerate(((1, low), (-1, high))):
            net.arrived(("first", k, s, m), r1.at[k, s, m], heavy(s, d))
            value = at(mix, k, s, (a + d + 4) % 4, half)[...] + r1[k, s, m].astype(F32)
            s1[k, s, 4 + m] = value.astype(BF16)
            net.start(("first", k, s, 4 + m), s1.at[k, s, 4 + m], r1.at[k, s, 4 + m], heavy(s, d))

    def scatter_light(k, s):
        a, b = here[s]
        for m in (2, 3, 4, 5):
            net.arrived(("first", k, s, m), r1.at[k, s, m], heavy(s, 1))
        for half, (m, n) in ((0, (4, 3)), (1, (2, 5))):
            own = at(mix, k, s, a, (low, high)[half])[...]
            t1[k, s, 2 * half : 2 * half + 2] = own + r1[k, s, m].astype(F32) + r1[k, s, n].astype(F32)
        for i, d in enumerate((1, -1, 2)):
            net.start(("second", k, s, i), t1.at[k, s, (b + d + 4) % 4], r2.at[k, s, i], light(s, d))

    def scatter_across(k, s):
        a, b = here[s]
        value = t1[k, s, b]
        for i in range(3):
            net.arrived(("second", k, s, i), r2.at[k, s, i], light(s, 1))
            value = value + r2[k, s, i]
        h = HALF_OF[k]
        if k in OTHER:
            t2[h, s] = value
            net.start(("third", h, s), t2.at[h, s], z3.at[h, s], across)
        else:
            net.arrived(("third", h, s), z3.at[h, s], across)
            out[16 * h : 16 * h + 16, 1024 * s : 1024 * s + 1024] = (value + z3[h, s]).astype(BF16)

    tasks = []

    def task(time, fn, *args):
        tasks.append((time, len(tasks), fn, args))

    for h in range(2):
        task(0, tokens_out, h)
    for k in range(CHUNKS):
        begin = (0.1, 3, 8, 13)[k]
        task(begin, tokens_light, k)
        for s in range(2):
            task(begin + 3.5, tokens_heavy, k, s)
            task(begin + 7, tokens_forward, k, s)
        ready = begin + 11
        for j in range(2):
            task(ready + 0.1 + 1.5 * j, multiply, k, j)
            piece = 14 + 3.5 * (2 * k + j)
            for p in range(4):
                task(piece + 4.5 * p, line, k, j, p)
            for p in (2, 1, 0):
                task(piece + 13.5 + 4 * (3 - p), back, k, j, p)
        task(ready, tokens_in, k)
        done = 14 + 3.5 * (2 * k + 1) + 28
        for s in range(2):
            task(done + 1 * s, project, k, s)
            task(done + 4 + 0.5 * s, scatter_sum, k, s)
            task(done + 8 + 0.5 * s, scatter_light, k, s)
            task(done + 12 + 0.5 * s + (10 if k == 0 else 0), scatter_across, k, s)
    for _, _, fn, args in sorted(tasks, key=lambda t: t[:2]):
        fn(*args)

    for k in range(CHUNKS):
        for j in range(2):
            lined = net.copy(("line", k, j), zs.at[k, :, columns(j)], zr.at[k, :, columns(j)], ahead)
            pl.when(pos < 3)(lined.wait_send)
            backed = net.copy(("back", k, j), block_of(k, j), block_of(k, j), behind)
            pl.when(pos > 0)(backed.wait_send)
            net.copy(("share", k, j), block_of(k, j), block_of(k, j), mate).wait_send()
    net.finish()


def on_device(tokens, gate_weight, up_weight, down_weight):
    hbm = pl.BlockSpec(memory_space=pl.ANY)
    n = CHUNKS
    return pl.pallas_call(
        kernel,
        out_shape=jax.ShapeDtypeStruct((32, 2048), BF16),
        in_specs=[hbm] * 4,
        out_specs=pl.BlockSpec(memory_space=pltpu.VMEM),
        scratch_shapes=[
            pltpu.VMEM((n, 4, 4, 16, 2048), BF16),
            pltpu.VMEM((2048, 1792), BF16),
            pltpu.VMEM((896, 2048), BF16),
            pltpu.VMEM((n, 2, 128, 1792), F32),
            pltpu.VMEM((n, 128, 1792), F32),
            pltpu.VMEM((n, 128, 1792), BF16),
            pltpu.VMEM((n, 128, 1792), BF16),
            pltpu.VMEM((n, 2, 128, 896), BF16),
            pltpu.VMEM((n, 4, 4, 16, 2048), F32),
            pltpu.VMEM((n, 2, 6, 2, 16, 1024), BF16),
            pltpu.VMEM((n, 2, 6, 2, 16, 1024), BF16),
            pltpu.VMEM((n, 2, 4, 16, 1024), WIDE),
            pltpu.VMEM((n, 2, 3, 16, 1024), WIDE),
            pltpu.VMEM((2, 2, 16, 1024), F32),
            pltpu.VMEM((2, 2, 16, 1024), F32),
            pltpu.SemaphoreType.DMA((17,)),
            pltpu.SemaphoreType.DMA((TRANSFERS,)),
            pltpu.SemaphoreType.DMA((TRANSFERS,)),
        ],
        compiler_params=pltpu.CompilerParams(
            collective_id=0, has_side_effects=True, vmem_limit_bytes=60 * 2**20
        ),
        name="panel",
    )(tokens, gate_weight, up_weight, down_weight)


def solution(mesh):
    return jax.shard_map(
        on_device,
        mesh=mesh,
        in_specs=(P("dp", "tensor"), P("tensor", "dp"), P("tensor", "dp"), P("dp", "tensor")),
        out_specs=P("dp", "tensor"),
        check_vma=False,
    )
```

```python
import jax
import jax.numpy as jnp
from jax import lax
from jax.experimental import pallas as pl
from jax.experimental.pallas import tpu as pltpu
from jax.sharding import PartitionSpec as P

F32, BF16 = jnp.float32, jnp.bfloat16
CHUNKS = 4
OWN, OTHER, HALF_OF = (0, 3), (1, 2), (0, 0, 1, 1)
SPLIT = ((0, 2), (2, 4), (4, 6), (6, 7))
MEET = ((1, 1, 1, 1), (1, 1, 1, 1), (1, 1, 1, 1), (1, 1, 1, 1))
GATHER_DIRECT = (1, 1, 1, 1)
SCATTER_DIRECT = (1, 1, 1, 1)
SECOND, THIRD = BF16, BF16
POOL = 48
PIECES = len(SPLIT)

ORDER = (
    (0, 0), (1, 0), (0, 1), (1, 3), (2, 0, 0), (2, 0, 1), (1, 1), (1, 2), (2, 3, 1), (2, 3, 0), (4, 0),
    (5, 0, 1), (5, 0, 0), (6, 0, 1, 0), (5, 0, 2), (2, 1, 0), (6, 0, 0, 0), (2, 1, 1), (6, 0, 2, 0), (5, 0, 3),
    (6, 0, 1, 1), (4, 3), (5, 3, 0), (5, 3, 3), (2, 2, 0), (6, 0, 3, 0), (2, 2, 1), (5, 3, 1), (6, 0, 2, 1),
    (6, 3, 0, 0), (5, 3, 2), (6, 0, 3, 1), (6, 3, 1, 0), (4, 1), (5, 1, 0), (6, 0, 0, 1), (6, 3, 3, 0),
    (5, 1, 2), (5, 1, 1), (6, 0, 1, 2), (7, 0, 1, 3), (6, 3, 2, 0), (6, 1, 0, 0), (6, 3, 0, 1), (5, 1, 3),
    (4, 2), (5, 2, 1), (6, 3, 1, 1), (6, 0, 2, 2), (6, 0, 0, 2), (6, 0, 3, 2), (5, 2, 3), (6, 1, 1, 0),
    (6, 3, 0, 2), (7, 0, 0, 3), (6, 3, 3, 1), (5, 2, 0), (6, 1, 3, 0), (6, 3, 1, 2), (6, 1, 2, 0), (5, 2, 2),
    (7, 0, 0, 1), (7, 0, 3, 1), (7, 0, 2, 1), (7, 0, 1, 1), (7, 0, 1, 0), (7, 0, 3, 0), (6, 3, 2, 1),
    (7, 3, 0, 1), (7, 3, 0, 0), (7, 0, 3, 3), (6, 1, 0, 1), (7, 0, 0, 0), (7, 0, 2, 0), (7, 0, 2, 3),
    (8, 0, 0), (6, 1, 1, 1), (6, 1, 3, 1), (6, 3, 3, 2), (7, 3, 3, 3), (6, 3, 2, 2), (7, 3, 2, 1),
    (6, 1, 0, 2), (7, 3, 1, 1), (6, 2, 0, 0), (6, 1, 2, 1), (8, 0, 1), (7, 3, 0, 3), (6, 2, 2, 0),
    (6, 2, 3, 0), (6, 2, 1, 0), (7, 3, 2, 0), (7, 3, 2, 3), (6, 1, 1, 2), (7, 3, 1, 3), (7, 3, 3, 1),
    (6, 1, 3, 2), (7, 3, 3, 0), (6, 1, 2, 2), (7, 3, 1, 0), (7, 1, 0, 1), (7, 1, 0, 0), (8, 3, 0),
    (6, 2, 0, 1), (6, 2, 3, 1), (6, 2, 2, 1), (7, 1, 1, 3), (8, 3, 1), (7, 1, 1, 1), (7, 1, 2, 3),
    (7, 1, 1, 0), (7, 1, 3, 1), (7, 1, 0, 3), (6, 2, 1, 1), (6, 2, 0, 2), (10, 0, 1), (6, 2, 3, 2),
    (6, 2, 2, 2), (7, 1, 3, 3), (7, 2, 3, 3), (6, 2, 1, 2), (7, 2, 2, 3), (7, 1, 2, 1), (7, 1, 2, 0),
    (7, 1, 3, 0), (7, 2, 0, 3), (8, 1, 0), (7, 2, 1, 3), (8, 1, 1), (7, 2, 3, 1), (7, 2, 3, 0), (7, 2, 0, 1),
    (7, 2, 2, 1), (7, 2, 0, 0), (7, 2, 2, 0), (7, 2, 1, 1), (7, 2, 1, 0), (8, 2, 0), (10, 1, 0), (8, 2, 1),
    (10, 1, 1), (10, 2, 0), (10, 3, 0), (11, 1, 0), (11, 1, 1), (10, 0, 0), (10, 2, 1), (11, 2, 0), (11, 2, 1),
    (10, 3, 1), (11, 0, 1), (11, 3, 0), (11, 0, 0), (11, 3, 1),
)


class Net:
    def __init__(self, send_sem, recv_sem):
        self.send_sem, self.recv_sem = send_sem, recv_sem
        self.arrivals, self.free, self.slots = {}, [], 0

    def take(self):
        if self.slots < POOL:
            self.slots += 1
            return self.slots - 1
        slot, one, when = self.free.pop(0)
        self.wait(one, when)
        return slot

    def give(self, slot, one, when=None):
        self.free.append((slot, one, when))

    def wait(self, one, when):
        if when is None:
            one.wait_send()
        else:
            pl.when(when)(one.wait_send)

    def copy(self, slot, name, src, dst, device):
        number = self.arrivals.setdefault(name, len(self.arrivals))
        return pltpu.make_async_remote_copy(
            src_ref=src,
            dst_ref=dst,
            send_sem=self.send_sem.at[slot],
            recv_sem=self.recv_sem.at[number],
            device_id=device,
            device_id_type=pl.DeviceIdType.MESH,
        )

    def start(self, name, src, dst, device):
        slot = self.take()
        one = self.copy(slot, name, src, dst, device)
        one.start()
        self.give(slot, one)

    def arrived(self, name, dst, device):
        assert name in self.arrivals
        self.copy(0, name, dst, dst, device).wait_recv()

    def finish(self):
        for _, one, when in self.free:
            self.wait(one, when)


ARRIVALS = 132


def kernel(tokens, gate, up, down, out, tok, wgu, wd, part, pair, zs, zr, hid, mix, s1, r1, t1, t1s, r2, t2, z3, local_sem, send_sem, recv_sem):
    dp, tensor = lax.axis_index("dp"), lax.axis_index("tensor")
    x, y, zh = dp // 8, (dp // 2) % 4, dp % 2
    zl, core = tensor // 2, tensor % 2
    pos = jnp.where(core == 0, zl, 3 - zl)
    step = jnp.where(core == 0, 1, -1)

    def plane(dx, dy):
        return ((((x + dx + 4) % 4) * 4 + (y + dy + 4) % 4) * 2 + zh, tensor)

    across = ((x * 4 + y) * 2 + 1 - zh, tensor)
    mate = (dp, zl * 2 + 1 - core)
    ahead = (dp, (zl + step) * 2 + core)
    behind = (dp, (zl - step) * 2 + core)

    def columns(j):
        return pl.ds(256 * SPLIT[j][0], 256 * (SPLIT[j][1] - SPLIT[j][0]))

    def units(j):
        return pl.ds(128 * SPLIT[j][0], 128 * (SPLIT[j][1] - SPLIT[j][0]))

    mine = [
        pltpu.make_async_copy(tokens.at[pl.ds(16 * h, 16)], tok.at[OWN[h], y, x], local_sem.at[h])
        for h in range(2)
    ]
    for one in mine:
        one.start()
    for j in range(PIECES):
        for n in range(*SPLIT[j]):
            for g, ref in enumerate((gate, up)):
                pltpu.make_async_copy(
                    ref.at[:, pl.ds(128 * n, 128)],
                    wgu.at[:, pl.ds(256 * n + 128 * g, 128)],
                    local_sem.at[2 + j],
                ).start()
    weights = [
        pltpu.make_async_copy(wgu.at[:, columns(j)], wgu.at[:, columns(j)], local_sem.at[2 + j])
        for j in range(PIECES)
    ]
    weights.append(pltpu.make_async_copy(down, wd, local_sem.at[2 + PIECES]))
    weights[-1].start()
    unread = set(range(PIECES + 1))

    def weight(j):
        if j in unread:
            unread.remove(j)
            weights[j].wait()

    barrier = pltpu.get_barrier_semaphore()

    def greet(device):
        pl.semaphore_signal(barrier, inc=1, device_id=device, device_id_type=pl.DeviceIdType.MESH)

    for dx, dy in ((1, 0), (-1, 0), (2, 0), (0, 1), (0, -1), (0, 2)):
        greet(plane(dx, dy))
    greet(across)
    greet(mate)
    pl.when(pos < 3)(lambda: greet(ahead))
    pl.when(pos > 0)(lambda: greet(behind))
    pl.semaphore_wait(barrier, 8 + jnp.where(pos < 3, 1, 0) + jnp.where(pos > 0, 1, 0))

    net = Net(send_sem, recv_sem)

    def light(s, d):
        return plane(d, 0) if s == 0 else plane(0, d)

    def heavy(s, d):
        return plane(0, d) if s == 0 else plane(d, 0)

    here = ((y, x), (x, y))

    def at(ref, k, s, a, b):
        cols = pl.ds(1024 * s, 1024)
        return ref.at[k, a, b, :, cols] if s == 0 else ref.at[k, b, a, :, cols]

    every, low, high, three = pl.ds(0, 4), pl.ds(0, 2), pl.ds(2, 2), pl.ds(0, 3)

    def tokens_out(h):
        mine[h].wait()
        net.start(("z", h), tok.at[OWN[h], y, x], tok.at[OTHER[h], y, x], across)

    def tokens_light(k):
        if k in OTHER:
            net.arrived(("z", HALF_OF[k]), tok.at[k, y, x], across)
        for s in range(2):
            a, b = here[s]
            block = at(tok, k, s, a, b)
            for d in (1, -1, 2):
                net.start(("light", k, s), block, block, light(s, d))

    def tokens_heavy(k, s):
        a, b = here[s]
        net.arrived(("light", k, s), at(tok, k, s, a, three), light(s, 1))
        line = at(tok, k, s, a, every)
        for d in (1, -1, 2) if GATHER_DIRECT[k] else (1, -1):
            net.start(("heavy", k, s), line, line, heavy(s, d))

    def tokens_forward(k, s):
        a, b = here[s]
        net.arrived(("heavy", k, s), at(tok, k, s, low, every), heavy(s, 1))
        for d, half in ((1, low), (-1, high)):
            block = at(tok, k, s, (a - d + 4) % 4, half)
            net.start(("forward", k, s), block, block, heavy(s, d))

    def tokens_in(k):
        for s in range(2):
            if GATHER_DIRECT[k]:
                net.arrived(("heavy", k, s), at(tok, k, s, three, every), heavy(s, 1))
            else:
                net.arrived(("forward", k, s), at(tok, k, s, 0, every), heavy(s, 1))

    def multiply(k, j):
        weight(j)

        @pl.loop(*SPLIT[j])
        def _(n):
            cols = pl.ds(pl.multiple_of(n * 256, 256), 256)
            value = jnp.dot(tok[k].reshape(256, 2048), wgu[:, cols], preferred_element_type=F32)
            part[k, :, :, cols] = value.reshape(2, 128, 256)

        net.start(("pair", k, j), part.at[k, 1 - core, :, columns(j)], pair.at[k, :, columns(j)], mate)

    def total(k, j, rows, *more):
        cols = columns(j)
        value = part[k, core, rows, cols] + pair[k, rows, cols]
        for ref in more:
            value = value + ref[k, rows, cols].astype(F32)
        return value

    held = {}

    def end(k, j):
        return 2 if MEET[k][j] else 3

    def line_copy(k, j, up):
        src = zs.at[k, :, columns(j)]
        if up:
            return net.copy(held["line", k, j], ("line", k, j), src, zr.at[k, :, columns(j)], ahead)
        return net.copy(held["line", k, j], ("down", k, j), src, src, behind)

    def pass_on(k, j, up, *more):
        @pl.loop(0, 8)
        def _(r):
            rows = pl.ds(pl.multiple_of(r * 16, 16), 16)
            zs[k, rows, columns(j)] = total(k, j, rows, *more).astype(BF16)

        line_copy(k, j, up).start()

    def hidden_copy(k, j, name):
        block = hid.at[k, core, :, units(j)]
        arrival = ("share", k) if name == "share" else ("back", k, j)
        device = {"share": mate, "back": behind, "onward": ahead}[name]
        return net.copy(held[name, k, j], arrival, block, block, device)

    def hidden_out(k, j, *names):
        for name in names:
            hidden_copy(k, j, name).start()

    def activate(k, j, *more):
        @pl.loop(0, 8)
        def _(r):
            rows = pl.ds(pl.multiple_of(r * 16, 16), 16)
            value = total(k, j, rows, *more)
            for n in range(SPLIT[j][1] - SPLIT[j][0]):
                g, u = value[:, 256 * n : 256 * n + 128], value[:, 256 * n + 128 : 256 * n + 256]
                unit = 128 * (SPLIT[j][0] + n)
                hid[k, core, rows, unit : unit + 128] = (g / (1.0 + jnp.exp(-g)) * u).astype(BF16)

    def line(k, j, p):
        if p == 0:
            held["line", k, j] = net.take()
            net.arrived(("pair", k, j), pair.at[k, :, columns(j)], mate)
        if p == end(k, j):
            for name in ("back", "share") + (("onward",) if MEET[k][j] else ()):
                held[name, k, j] = net.take()

        def go():
            if p == 0:
                pass_on(k, j, True)
                return
            net.arrived(("line", k, j), zr.at[k, :, columns(j)], behind)
            if p < end(k, j):
                pass_on(k, j, True, zr)
            elif MEET[k][j]:
                net.arrived(("down", k, j), zs.at[k, :, columns(j)], ahead)
                activate(k, j, zr, zs)
                hidden_out(k, j, "back", "onward", "share")
            else:
                activate(k, j, zr)
                hidden_out(k, j, "back", "share")

        pl.when(pos == p)(go)
        if p == 0 and MEET[k][j]:
            pl.when(pos == 3)(lambda: pass_on(k, j, False))
        if p == end(k, j) - 1:
            net.give(held["line", k, j], line_copy(k, j, True), pos != end(k, j))

    backs = {}

    def back(k, j, p):
        def go():
            net.arrived(("back", k, j), hid.at[k, core, :, units(j)], ahead if p < end(k, j) else behind)
            hidden_out(k, j, *(("back",) if p and p < end(k, j) else ()), "share")

        pl.when(pos == p)(go)
        backs[k, j] = backs.get((k, j), 0) + 1
        if backs[k, j] == 3:
            senders = (pos == 1) | (pos == 2) if MEET[k][j] else pos > 0
            net.give(held["back", k, j], hidden_copy(k, j, "back"), senders)
            net.give(held["share", k, j], hidden_copy(k, j, "share"))
            if MEET[k][j]:
                net.give(held["onward", k, j], hidden_copy(k, j, "onward"), pos == 2)

    def project(k, s):
        if s == 0:
            weight(PIECES)
            net.arrived(("share", k), hid.at[k, 1 - core], mate)

        @pl.loop(4 * s, 4 * s + 4)
        def _(n):
            cols = pl.ds(pl.multiple_of(n * 256, 256), 256)
            value = jnp.dot(hid[k].reshape(256, 896), wd[:, cols], preferred_element_type=F32)
            mix[k, :, :, :, cols] = value.reshape(4, 4, 16, 256)

        a, b = here[s]
        if SCATTER_DIRECT[k]:
            for i, d in enumerate((1, -1, 2)):
                s1[k, s, i] = at(mix, k, s, (a + d + 4) % 4, every)[...].astype(BF16)
                net.start(("last", k, s), s1.at[k, s, i], r1.at[k, s, i], heavy(s, d))
            return
        sends = ((0, low, 2, 1, low), (0, high, 2, -1, high), (1, high, 1, 1, high), (2, low, -1, -1, low))
        for i, place, to, d, half in sends:
            s1[k, s, i, place] = at(mix, k, s, (a + to + 4) % 4, half)[...].astype(BF16)
            name = "first" if i == 0 else "last"
            net.start((name, k, s), s1.at[k, s, i, place], r1.at[k, s, i, place], heavy(s, d))

    def scatter_sum(k, s):
        a, b = here[s]
        net.arrived(("first", k, s), r1.at[k, s, 0], heavy(s, 1))
        for i, half, d in ((1, low, 1), (2, high, -1)):
            value = at(mix, k, s, (a + d + 4) % 4, half)[...] + r1[k, s, 0, half].astype(F32)
            s1[k, s, i, half] = value.astype(BF16)
            net.start(("last", k, s), s1.at[k, s, i, half], r1.at[k, s, i, half], heavy(s, d))

    def scatter_light(k, s):
        a, b = here[s]
        value = at(mix, k, s, a, every)[...]
        if SCATTER_DIRECT[k]:
            net.arrived(("last", k, s), r1.at[k, s], heavy(s, 1))
            value = value + r1[k, s, 0].astype(F32)
        else:
            net.arrived(("last", k, s), r1.at[k, s, pl.ds(1, 2)], heavy(s, 1))
        value = value + r1[k, s, 1].astype(F32) + r1[k, s, 2].astype(F32)
        t1[k, s] = value
        t1s[k, s] = value.astype(SECOND)
        for i, d in enumerate((1, -1, 2)):
            net.start(("second", k, s), t1s.at[k, s, (b + d + 4) % 4], r2.at[k, s, i], light(s, d))

    def scatter_across(k, s):
        a, b = here[s]
        net.arrived(("second", k, s), r2.at[k, s], light(s, 1))
        value = t1[k, s, b]
        for i in range(3):
            value = value + r2[k, s, i].astype(F32)
        h = HALF_OF[k]
        if k in OTHER:
            t2[h, s] = value.astype(THIRD)
            net.start(("third", h, s), t2.at[h, s], z3.at[h, s], across)
        else:
            net.arrived(("third", h, s), z3.at[h, s], across)
            out[16 * h : 16 * h + 16, 1024 * s : 1024 * s + 1024] = (value + z3[h, s].astype(F32)).astype(BF16)

    STEPS = (
        tokens_out, tokens_light, tokens_heavy, tokens_forward, tokens_in, multiply,
        line, back, project, scatter_sum, scatter_light, scatter_across,
    )
    for number, *args in ORDER:
        STEPS[number](*args)
    net.finish()


def on_device(tokens, gate_weight, up_weight, down_weight):
    hbm = pl.BlockSpec(memory_space=pl.ANY)
    n = CHUNKS
    return pl.pallas_call(
        kernel,
        out_shape=jax.ShapeDtypeStruct((32, 2048), BF16),
        in_specs=[hbm] * 4,
        out_specs=pl.BlockSpec(memory_space=pltpu.VMEM),
        scratch_shapes=[
            pltpu.VMEM((n, 4, 4, 16, 2048), BF16),
            pltpu.VMEM((2048, 1792), BF16),
            pltpu.VMEM((896, 2048), BF16),
            pltpu.VMEM((n, 2, 128, 1792), F32),
            pltpu.VMEM((n, 128, 1792), F32),
            pltpu.VMEM((n, 128, 1792), BF16),
            pltpu.VMEM((n, 128, 1792), BF16),
            pltpu.VMEM((n, 2, 128, 896), BF16),
            pltpu.VMEM((n, 4, 4, 16, 2048), F32),
            pltpu.VMEM((n, 2, 3, 4, 16, 1024), BF16),
            pltpu.VMEM((n, 2, 3, 4, 16, 1024), BF16),
            pltpu.VMEM((n, 2, 4, 16, 1024), F32),
            pltpu.VMEM((n, 2, 4, 16, 1024), SECOND),
            pltpu.VMEM((n, 2, 3, 16, 1024), SECOND),
            pltpu.VMEM((2, 2, 16, 1024), THIRD),
            pltpu.VMEM((2, 2, 16, 1024), THIRD),
            pltpu.SemaphoreType.DMA((3 + PIECES,)),
            pltpu.SemaphoreType.DMA((POOL,)),
            pltpu.SemaphoreType.DMA((ARRIVALS,)),
        ],
        compiler_params=pltpu.CompilerParams(
            collective_id=0, has_side_effects=True, vmem_limit_bytes=60 * 2**20
        ),
        name="panel",
    )(tokens, gate_weight, up_weight, down_weight)


def solution(mesh):
    return jax.shard_map(
        on_device,
        mesh=mesh,
        in_specs=(P("dp", "tensor"), P("tensor", "dp"), P("tensor", "dp"), P("dp", "tensor")),
        out_specs=P("dp", "tensor"),
        check_vma=False,
    )
```

```python
import jax
import jax.numpy as jnp
from jax import lax
from jax.experimental import pallas as pl
from jax.experimental.pallas import tpu as pltpu
from jax.sharding import PartitionSpec as P

F32, BF16 = jnp.float32, jnp.bfloat16
CHUNKS = 4
OWN, OTHER, HALF_OF = (0, 3), (1, 2), (0, 0, 1, 1)
SPLIT = ((0, 2), (2, 4), (4, 6), (6, 7))
MEET = ((1, 1, 1, 1), (1, 1, 1, 1), (1, 1, 1, 1), (1, 1, 1, 1))
GATHER_DIRECT = (1, 1, 1, 1)
SCATTER_DIRECT = (0, 0, 1, 1)
PROJECT_EARLY = (0, 0, 0, 0)
SECOND, THIRD = BF16, BF16
POOL = 48
PIECES = len(SPLIT)

ORDER = (
    (0, 0), (1, 0), (2, 0, 1), (2, 0, 0), (0, 1), (1, 1), (1, 2), (4, 0), (5, 0, 2), (2, 1, 1), (2, 1, 0),
    (5, 0, 0), (6, 0, 0, 0), (5, 0, 1), (6, 0, 0, 1), (6, 0, 2, 0), (6, 0, 2, 1), (1, 3), (2, 2, 1), (5, 0, 3),
    (2, 2, 0), (4, 1), (5, 1, 3), (6, 0, 1, 0), (5, 1, 0), (5, 1, 2), (6, 0, 0, 2), (6, 0, 3, 0), (5, 1, 1),
    (6, 0, 1, 1), (7, 0, 0, 3), (2, 3, 1), (2, 3, 0), (6, 1, 0, 0), (6, 0, 3, 1), (6, 1, 0, 1), (6, 1, 2, 0),
    (6, 1, 2, 1), (6, 1, 3, 0), (6, 0, 2, 2), (6, 1, 3, 1), (4, 2), (5, 2, 0), (5, 2, 2), (6, 1, 1, 0),
    (6, 1, 1, 1), (5, 2, 3), (6, 0, 1, 2), (5, 2, 1), (6, 1, 0, 2), (7, 1, 0, 3), (7, 0, 2, 1), (6, 0, 3, 2),
    (4, 3), (5, 3, 0), (6, 1, 2, 2), (7, 0, 2, 3), (6, 2, 2, 0), (5, 3, 1), (7, 0, 1, 1), (7, 1, 0, 1),
    (6, 2, 2, 1), (6, 2, 0, 0), (7, 1, 2, 3), (6, 1, 3, 2), (7, 1, 3, 3), (6, 2, 3, 0), (7, 0, 1, 3),
    (6, 2, 1, 0), (5, 3, 3), (7, 0, 3, 1), (6, 1, 1, 2), (7, 1, 1, 3), (5, 3, 2), (7, 1, 2, 1), (6, 2, 2, 2),
    (7, 2, 2, 3), (6, 3, 1, 0), (6, 3, 3, 0), (6, 2, 3, 1), (6, 2, 3, 2), (6, 3, 0, 0), (7, 1, 2, 0),
    (7, 1, 0, 0), (6, 2, 0, 1), (7, 1, 3, 1), (7, 0, 0, 1), (6, 3, 2, 0), (7, 1, 1, 1), (7, 1, 1, 0),
    (7, 0, 3, 3), (6, 2, 0, 2), (6, 2, 1, 1), (6, 2, 1, 2), (7, 0, 0, 0), (7, 1, 3, 0), (8, 1, 0), (8, 1, 1),
    (7, 2, 1, 3), (7, 0, 2, 0), (7, 2, 0, 3), (7, 0, 3, 0), (7, 2, 3, 3), (7, 0, 1, 0), (8, 0, 0), (8, 0, 1),
    (6, 3, 1, 1), (7, 2, 2, 1), (6, 3, 3, 1), (6, 3, 3, 2), (6, 3, 1, 2), (7, 2, 0, 1), (7, 2, 1, 1),
    (7, 2, 3, 1), (6, 3, 0, 1), (6, 3, 0, 2), (7, 2, 2, 0), (6, 3, 2, 1), (9, 1, 0), (6, 3, 2, 2), (9, 1, 1),
    (7, 2, 0, 0), (7, 2, 1, 0), (7, 2, 3, 0), (8, 2, 0), (8, 2, 1), (7, 3, 3, 3), (9, 0, 1), (7, 3, 2, 3),
    (9, 0, 0), (7, 3, 1, 1), (7, 3, 1, 0), (7, 3, 3, 1), (7, 3, 0, 1), (7, 3, 1, 3), (7, 3, 0, 3), (10, 1, 0),
    (10, 1, 1), (7, 3, 3, 0), (7, 3, 2, 1), (7, 3, 2, 0), (10, 2, 0), (10, 2, 1), (7, 3, 0, 0), (8, 3, 0),
    (8, 3, 1), (11, 1, 0), (11, 2, 1), (11, 1, 1), (11, 2, 0), (10, 0, 1), (10, 0, 0), (10, 3, 0), (10, 3, 1),
    (11, 0, 0), (11, 0, 1), (11, 3, 0), (11, 3, 1),
)


class Net:
    def __init__(self, send_sem, recv_sem):
        self.send_sem, self.recv_sem = send_sem, recv_sem
        self.arrivals, self.free, self.slots = {}, [], 0

    def take(self):
        if self.slots < POOL:
            self.slots += 1
            return self.slots - 1
        slot, one, when = self.free.pop(0)
        self.wait(one, when)
        return slot

    def give(self, slot, one, when=None):
        self.free.append((slot, one, when))

    def wait(self, one, when):
        if when is None:
            one.wait_send()
        else:
            pl.when(when)(one.wait_send)

    def copy(self, slot, name, src, dst, device):
        number = self.arrivals.setdefault(name, len(self.arrivals))
        return pltpu.make_async_remote_copy(
            src_ref=src,
            dst_ref=dst,
            send_sem=self.send_sem.at[slot],
            recv_sem=self.recv_sem.at[number],
            device_id=device,
            device_id_type=pl.DeviceIdType.MESH,
        )

    def start(self, name, src, dst, device):
        slot = self.take()
        one = self.copy(slot, name, src, dst, device)
        one.start()
        self.give(slot, one)

    def arrived(self, name, dst, device):
        assert name in self.arrivals
        self.copy(0, name, dst, dst, device).wait_recv()

    def finish(self):
        for _, one, when in self.free:
            self.wait(one, when)


ARRIVALS = 132


def kernel(tokens, gate, up, down, out, tok, wgu, wd, part, pair, zs, zr, hid, mix, s1, r1, t1, t1s, r2, t2, z3, local_sem, send_sem, recv_sem):
    dp, tensor = lax.axis_index("dp"), lax.axis_index("tensor")
    x, y, zh = dp // 8, (dp // 2) % 4, dp % 2
    zl, core = tensor // 2, tensor % 2
    pos = jnp.where(core == 0, zl, 3 - zl)
    step = jnp.where(core == 0, 1, -1)

    def plane(dx, dy):
        return ((((x + dx + 4) % 4) * 4 + (y + dy + 4) % 4) * 2 + zh, tensor)

    across = ((x * 4 + y) * 2 + 1 - zh, tensor)
    mate = (dp, zl * 2 + 1 - core)
    ahead = (dp, (zl + step) * 2 + core)
    behind = (dp, (zl - step) * 2 + core)

    def columns(j):
        return pl.ds(256 * SPLIT[j][0], 256 * (SPLIT[j][1] - SPLIT[j][0]))

    def units(j):
        return pl.ds(128 * SPLIT[j][0], 128 * (SPLIT[j][1] - SPLIT[j][0]))

    mine = [
        pltpu.make_async_copy(tokens.at[pl.ds(16 * h, 16)], tok.at[OWN[h], y, x], local_sem.at[h])
        for h in range(2)
    ]
    for one in mine:
        one.start()
    for j in range(PIECES):
        for n in range(*SPLIT[j]):
            for g, ref in enumerate((gate, up)):
                pltpu.make_async_copy(
                    ref.at[:, pl.ds(128 * n, 128)],
                    wgu.at[:, pl.ds(256 * n + 128 * g, 128)],
                    local_sem.at[2 + j],
                ).start()
    weights = [
        pltpu.make_async_copy(wgu.at[:, columns(j)], wgu.at[:, columns(j)], local_sem.at[2 + j])
        for j in range(PIECES)
    ]
    weights.append(pltpu.make_async_copy(down, wd, local_sem.at[2 + PIECES]))
    weights[-1].start()
    unread = set(range(PIECES + 1))

    def weight(j):
        if j in unread:
            unread.remove(j)
            weights[j].wait()

    barrier = pltpu.get_barrier_semaphore()

    def greet(device):
        pl.semaphore_signal(barrier, inc=1, device_id=device, device_id_type=pl.DeviceIdType.MESH)

    for dx, dy in ((1, 0), (-1, 0), (2, 0), (0, 1), (0, -1), (0, 2)):
        greet(plane(dx, dy))
    greet(across)
    greet(mate)
    pl.when(pos < 3)(lambda: greet(ahead))
    pl.when(pos > 0)(lambda: greet(behind))
    pl.semaphore_wait(barrier, 8 + jnp.where(pos < 3, 1, 0) + jnp.where(pos > 0, 1, 0))

    net = Net(send_sem, recv_sem)

    def light(s, d):
        return plane(d, 0) if s == 0 else plane(0, d)

    def heavy(s, d):
        return plane(0, d) if s == 0 else plane(d, 0)

    here = ((y, x), (x, y))

    def at(ref, k, s, a, b):
        cols = pl.ds(1024 * s, 1024)
        return ref.at[k, a, b, :, cols] if s == 0 else ref.at[k, b, a, :, cols]

    every, low, high, three = pl.ds(0, 4), pl.ds(0, 2), pl.ds(2, 2), pl.ds(0, 3)

    def tokens_out(h):
        mine[h].wait()
        net.start(("z", h), tok.at[OWN[h], y, x], tok.at[OTHER[h], y, x], across)

    def tokens_light(k):
        if k in OTHER:
            net.arrived(("z", HALF_OF[k]), tok.at[k, y, x], across)
        for s in range(2):
            a, b = here[s]
            block = at(tok, k, s, a, b)
            for d in (1, -1, 2):
                net.start(("light", k, s), block, block, light(s, d))

    def tokens_heavy(k, s):
        a, b = here[s]
        net.arrived(("light", k, s), at(tok, k, s, a, three), light(s, 1))
        line = at(tok, k, s, a, every)
        for d in (1, -1, 2) if GATHER_DIRECT[k] else (1, -1):
            net.start(("heavy", k, s), line, line, heavy(s, d))

    def tokens_forward(k, s):
        a, b = here[s]
        net.arrived(("heavy", k, s), at(tok, k, s, low, every), heavy(s, 1))
        for d, half in ((1, low), (-1, high)):
            block = at(tok, k, s, (a - d + 4) % 4, half)
            net.start(("forward", k, s), block, block, heavy(s, d))

    def tokens_in(k):
        for s in range(2):
            if GATHER_DIRECT[k]:
                net.arrived(("heavy", k, s), at(tok, k, s, three, every), heavy(s, 1))
            else:
                net.arrived(("forward", k, s), at(tok, k, s, 0, every), heavy(s, 1))

    def multiply(k, j):
        weight(j)

        @pl.loop(*SPLIT[j])
        def _(n):
            cols = pl.ds(pl.multiple_of(n * 256, 256), 256)
            value = jnp.dot(tok[k].reshape(256, 2048), wgu[:, cols], preferred_element_type=F32)
            part[k, :, :, cols] = value.reshape(2, 128, 256)

        net.start(("pair", k, j), part.at[k, 1 - core, :, columns(j)], pair.at[k, :, columns(j)], mate)

    def total(k, j, rows, *more):
        cols = columns(j)
        value = part[k, core, rows, cols] + pair[k, rows, cols]
        for ref in more:
            value = value + ref[k, rows, cols].astype(F32)
        return value

    held = {}

    def end(k, j):
        return 2 if MEET[k][j] else 3

    def line_copy(k, j, up):
        src = zs.at[k, :, columns(j)]
        if up:
            return net.copy(held["line", k, j], ("line", k, j), src, zr.at[k, :, columns(j)], ahead)
        return net.copy(held["line", k, j], ("down", k, j), src, src, behind)

    def pass_on(k, j, up, *more):
        @pl.loop(0, 8)
        def _(r):
            rows = pl.ds(pl.multiple_of(r * 16, 16), 16)
            zs[k, rows, columns(j)] = total(k, j, rows, *more).astype(BF16)

        line_copy(k, j, up).start()

    def hidden_copy(k, j, name):
        block = hid.at[k, core, :, units(j)]
        apart = bool(PROJECT_EARLY[k]) and j == PIECES - 1
        arrival = ("share", k, apart) if name == "share" else ("back", k, j)
        device = {"share": mate, "back": behind, "onward": ahead}[name]
        return net.copy(held[name, k, j], arrival, block, block, device)

    def hidden_out(k, j, *names):
        for name in names:
            hidden_copy(k, j, name).start()

    def activate(k, j, *more):
        @pl.loop(0, 8)
        def _(r):
            rows = pl.ds(pl.multiple_of(r * 16, 16), 16)
            value = total(k, j, rows, *more)
            for n in range(SPLIT[j][1] - SPLIT[j][0]):
                g, u = value[:, 256 * n : 256 * n + 128], value[:, 256 * n + 128 : 256 * n + 256]
                unit = 128 * (SPLIT[j][0] + n)
                hid[k, core, rows, unit : unit + 128] = (g / (1.0 + jnp.exp(-g)) * u).astype(BF16)

    def line(k, j, p):
        if p == 0:
            held["line", k, j] = net.take()
            net.arrived(("pair", k, j), pair.at[k, :, columns(j)], mate)
        if p == end(k, j):
            for name in ("back", "share") + (("onward",) if MEET[k][j] else ()):
                held[name, k, j] = net.take()

        def go():
            if p == 0:
                pass_on(k, j, True)
                return
            net.arrived(("line", k, j), zr.at[k, :, columns(j)], behind)
            if p < end(k, j):
                pass_on(k, j, True, zr)
            elif MEET[k][j]:
                net.arrived(("down", k, j), zs.at[k, :, columns(j)], ahead)
                activate(k, j, zr, zs)
                hidden_out(k, j, "back", "onward", "share")
            else:
                activate(k, j, zr)
                hidden_out(k, j, "back", "share")

        pl.when(pos == p)(go)
        if p == 0 and MEET[k][j]:
            pl.when(pos == 3)(lambda: pass_on(k, j, False))
        if p == end(k, j) - 1:
            net.give(held["line", k, j], line_copy(k, j, True), pos != end(k, j))

    backs = {}

    def back(k, j, p):
        def go():
            net.arrived(("back", k, j), hid.at[k, core, :, units(j)], ahead if p < end(k, j) else behind)
            hidden_out(k, j, *(("back",) if p and p < end(k, j) else ()), "share")

        pl.when(pos == p)(go)
        backs[k, j] = backs.get((k, j), 0) + 1
        if backs[k, j] == 3:
            senders = (pos == 1) | (pos == 2) if MEET[k][j] else pos > 0
            net.give(held["back", k, j], hidden_copy(k, j, "back"), senders)
            net.give(held["share", k, j], hidden_copy(k, j, "share"))
            if MEET[k][j]:
                net.give(held["onward", k, j], hidden_copy(k, j, "onward"), pos == 2)

    def down_product(k, s, first, last, more):
        if s == 0:
            weight(PIECES)
            part_of = (k, 1 - core, slice(None), pl.ds(first, last - first))
            net.arrived(("share", k, more), hid.at[part_of], mate)

        @pl.loop(4 * s, 4 * s + 4)
        def _(n):
            cols = pl.ds(pl.multiple_of(n * 256, 256), 256)
            value = jnp.dot(
                hid[k, :, :, first:last].reshape(256, last - first), wd[first:last, cols], preferred_element_type=F32
            ).reshape(4, 4, 16, 256)
            mix[k, :, :, :, cols] = mix[k, :, :, :, cols] + value if more else value

    def begin(k, s):
        down_product(k, s, 0, 128 * SPLIT[-1][0], False)

    def project(k, s):
        early = PROJECT_EARLY[k]
        down_product(k, s, 128 * SPLIT[-1][0] if early else 0, 896, bool(early))
        a, b = here[s]
        if SCATTER_DIRECT[k]:
            for i, d in enumerate((1, -1, 2)):
                s1[k, s, i] = at(mix, k, s, (a + d + 4) % 4, every)[...].astype(BF16)
                net.start(("last", k, s), s1.at[k, s, i], r1.at[k, s, i], heavy(s, d))
            return
        sends = ((0, low, 2, 1, low), (0, high, 2, -1, high), (1, high, 1, 1, high), (2, low, -1, -1, low))
        for i, place, to, d, half in sends:
            s1[k, s, i, place] = at(mix, k, s, (a + to + 4) % 4, half)[...].astype(BF16)
            name = "first" if i == 0 else "last"
            net.start((name, k, s), s1.at[k, s, i, place], r1.at[k, s, i, place], heavy(s, d))

    def scatter_sum(k, s):
        a, b = here[s]
        net.arrived(("first", k, s), r1.at[k, s, 0], heavy(s, 1))
        for i, half, d in ((1, low, 1), (2, high, -1)):
            value = at(mix, k, s, (a + d + 4) % 4, half)[...] + r1[k, s, 0, half].astype(F32)
            s1[k, s, i, half] = value.astype(BF16)
            net.start(("last", k, s), s1.at[k, s, i, half], r1.at[k, s, i, half], heavy(s, d))

    def scatter_light(k, s):
        a, b = here[s]
        value = at(mix, k, s, a, every)[...]
        if SCATTER_DIRECT[k]:
            net.arrived(("last", k, s), r1.at[k, s], heavy(s, 1))
            value = value + r1[k, s, 0].astype(F32)
        else:
            net.arrived(("last", k, s), r1.at[k, s, pl.ds(1, 2)], heavy(s, 1))
        value = value + r1[k, s, 1].astype(F32) + r1[k, s, 2].astype(F32)
        t1[k, s] = value
        t1s[k, s] = value.astype(SECOND)
        for i, d in enumerate((1, -1, 2)):
            net.start(("second", k, s), t1s.at[k, s, (b + d + 4) % 4], r2.at[k, s, i], light(s, d))

    def scatter_across(k, s):
        a, b = here[s]
        net.arrived(("second", k, s), r2.at[k, s], light(s, 1))
        value = t1[k, s, b]
        for i in range(3):
            value = value + r2[k, s, i].astype(F32)
        h = HALF_OF[k]
        if k in OTHER:
            t2[h, s] = value.astype(THIRD)
            net.start(("third", h, s), t2.at[h, s], z3.at[h, s], across)
        else:
            net.arrived(("third", h, s), z3.at[h, s], across)
            out[16 * h : 16 * h + 16, 1024 * s : 1024 * s + 1024] = (value + z3[h, s].astype(F32)).astype(BF16)

    STEPS = (
        tokens_out, tokens_light, tokens_heavy, tokens_forward, tokens_in, multiply,
        line, back, project, scatter_sum, scatter_light, scatter_across, begin,
    )
    for number, *args in ORDER:
        STEPS[number](*args)
    net.finish()


def on_device(tokens, gate_weight, up_weight, down_weight):
    hbm = pl.BlockSpec(memory_space=pl.ANY)
    n = CHUNKS
    return pl.pallas_call(
        kernel,
        out_shape=pltpu.VMEM((32, 2048), BF16),
        in_specs=[hbm] * 4,
        out_specs=pl.BlockSpec(memory_space=pltpu.VMEM),
        scratch_shapes=[
            pltpu.VMEM((n, 4, 4, 16, 2048), BF16),
            pltpu.VMEM((2048, 1792), BF16),
            pltpu.VMEM((896, 2048), BF16),
            pltpu.VMEM((n, 2, 128, 1792), F32),
            pltpu.VMEM((n, 128, 1792), F32),
            pltpu.VMEM((n, 128, 1792), BF16),
            pltpu.VMEM((n, 128, 1792), BF16),
            pltpu.VMEM((n, 2, 128, 896), BF16),
            pltpu.VMEM((n, 4, 4, 16, 2048), F32),
            pltpu.VMEM((n, 2, 3, 4, 16, 1024), BF16),
            pltpu.VMEM((n, 2, 3, 4, 16, 1024), BF16),
            pltpu.VMEM((n, 2, 4, 16, 1024), F32),
            pltpu.VMEM((n, 2, 4, 16, 1024), SECOND),
            pltpu.VMEM((n, 2, 3, 16, 1024), SECOND),
            pltpu.VMEM((2, 2, 16, 1024), THIRD),
            pltpu.VMEM((2, 2, 16, 1024), THIRD),
            pltpu.SemaphoreType.DMA((3 + PIECES,)),
            pltpu.SemaphoreType.DMA((POOL,)),
            pltpu.SemaphoreType.DMA((ARRIVALS,)),
        ],
        compiler_params=pltpu.CompilerParams(
            collective_id=0, has_side_effects=True, vmem_limit_bytes=60 * 2**20
        ),
        name="panel",
    )(tokens, gate_weight, up_weight, down_weight)


def solution(mesh):
    return jax.shard_map(
        on_device,
        mesh=mesh,
        in_specs=(P("dp", "tensor"), P("tensor", "dp"), P("tensor", "dp"), P("dp", "tensor")),
        out_specs=P("dp", "tensor"),
        check_vma=False,
    )
```

```python
import jax
import jax.numpy as jnp
from jax import lax
from jax.experimental import pallas as pl
from jax.experimental.pallas import tpu as pltpu
from jax.sharding import PartitionSpec as P

F32, BF16 = jnp.float32, jnp.bfloat16
GROUPS = 4
OWN, OTHER, HALF_OF = (0, 3), (1, 2), (0, 0, 1, 1)
CHUNKS = 8
SPLIT = ((0, 4), (4, 7))
MEET = ((1, 1), (1, 1), (1, 1), (1, 1), (1, 1), (1, 1), (1, 1), (1, 1))
POOL = 40
PIECES = len(SPLIT)

ORDER = (
    (0, 1), (0, 0), (1, 0), (1, 3), (2, 1, 0), (2, 1, 1), (1, 2), (2, 0, 1), (2, 0, 0), (4, 1), (5, 1, 1),
    (1, 1), (5, 1, 0), (2, 4, 1), (2, 4, 0), (6, 1, 1, 0), (2, 5, 1), (4, 0), (5, 0, 0), (6, 1, 0, 0),
    (2, 5, 0), (2, 2, 0), (6, 1, 1, 1), (5, 0, 1), (2, 7, 0), (2, 3, 0), (2, 2, 1), (6, 1, 0, 1), (4, 4),
    (2, 3, 1), (6, 0, 0, 0), (5, 4, 1), (5, 4, 0), (6, 1, 1, 2), (2, 7, 1), (6, 0, 0, 1), (4, 5), (6, 0, 1, 0),
    (2, 6, 1), (5, 5, 1), (7, 1, 1, 1), (6, 4, 1, 0), (5, 5, 0), (2, 6, 0), (6, 4, 0, 0), (6, 1, 0, 2), (4, 2),
    (6, 4, 1, 1), (5, 2, 1), (7, 1, 1, 3), (6, 0, 1, 1), (5, 2, 0), (6, 5, 1, 0), (7, 1, 0, 1), (6, 4, 0, 1),
    (4, 3), (5, 3, 0), (6, 0, 0, 2), (5, 3, 1), (6, 5, 0, 0), (6, 4, 1, 2), (6, 2, 0, 0), (7, 1, 0, 3),
    (6, 5, 1, 1), (6, 2, 1, 0), (6, 5, 0, 1), (4, 7), (7, 0, 0, 1), (7, 4, 1, 1), (5, 7, 1), (6, 4, 0, 2),
    (6, 2, 0, 1), (6, 0, 1, 2), (5, 7, 0), (7, 0, 0, 3), (7, 4, 1, 3), (7, 4, 0, 1), (4, 6), (7, 0, 1, 1),
    (6, 2, 1, 1), (6, 5, 1, 2), (7, 1, 1, 0), (7, 4, 0, 3), (5, 6, 1), (5, 6, 0), (7, 5, 1, 1), (7, 0, 1, 3),
    (7, 5, 1, 3), (7, 1, 0, 0), (6, 3, 1, 0), (6, 5, 0, 2), (8, 1, 0), (6, 3, 1, 1), (6, 3, 0, 0),
    (7, 5, 0, 1), (6, 3, 0, 1), (6, 2, 0, 2), (6, 7, 0, 0), (7, 5, 0, 3), (8, 1, 1), (6, 7, 1, 0),
    (7, 2, 0, 3), (6, 2, 1, 2), (7, 0, 0, 0), (7, 2, 0, 1), (6, 6, 1, 0), (6, 7, 0, 1), (6, 6, 0, 0),
    (7, 4, 0, 0), (7, 4, 1, 0), (7, 0, 1, 0), (8, 4, 0), (7, 2, 1, 1), (8, 4, 1), (6, 7, 1, 1), (7, 5, 1, 0),
    (8, 0, 0), (7, 2, 1, 3), (6, 6, 1, 1), (8, 0, 1), (6, 3, 1, 2), (7, 5, 0, 0), (8, 5, 0), (8, 5, 1),
    (6, 3, 0, 2), (7, 3, 1, 1), (7, 3, 1, 3), (6, 6, 0, 1), (7, 3, 0, 1), (6, 7, 0, 2), (7, 2, 0, 0),
    (7, 2, 1, 0), (8, 2, 0), (7, 3, 0, 3), (7, 7, 0, 3), (8, 2, 1), (7, 7, 0, 1), (7, 3, 1, 0), (6, 7, 1, 2),
    (7, 7, 1, 1), (7, 3, 0, 0), (7, 7, 1, 3), (6, 6, 1, 2), (7, 6, 1, 3), (8, 3, 0), (7, 6, 1, 1), (8, 3, 1),
    (7, 7, 0, 0), (6, 6, 0, 2), (10, 2, 0), (7, 6, 0, 1), (10, 2, 1), (7, 7, 1, 0), (8, 7, 0), (8, 7, 1),
    (7, 6, 0, 3), (10, 1, 1), (10, 1, 0), (7, 6, 1, 0), (11, 2, 0), (7, 6, 0, 0), (8, 6, 0), (8, 6, 1),
    (10, 0, 1), (11, 1, 0), (10, 0, 0), (11, 2, 1), (11, 1, 1), (10, 3, 0), (10, 3, 1), (11, 0, 0), (11, 0, 1),
    (11, 3, 0), (11, 3, 1),
)


class Net:
    def __init__(self, send_sem, recv_sem):
        self.send_sem, self.recv_sem = send_sem, recv_sem
        self.arrivals, self.free, self.slots = {}, [], 0

    def take(self):
        if self.slots < POOL:
            self.slots += 1
            return self.slots - 1
        slot, one, when = self.free.pop(0)
        self.wait(one, when)
        return slot

    def give(self, slot, one, when=None):
        self.free.append((slot, one, when))

    def wait(self, one, when):
        if when is None:
            one.wait_send()
        else:
            pl.when(when)(one.wait_send)

    def copy(self, slot, name, src, dst, device):
        number = self.arrivals.setdefault(name, len(self.arrivals))
        return pltpu.make_async_remote_copy(
            src_ref=src,
            dst_ref=dst,
            send_sem=self.send_sem.at[slot],
            recv_sem=self.recv_sem.at[number],
            device_id=device,
            device_id_type=pl.DeviceIdType.MESH,
        )

    def start(self, name, src, dst, device):
        slot = self.take()
        one = self.copy(slot, name, src, dst, device)
        one.start()
        self.give(slot, one)

    def arrived(self, name, dst, device):
        assert name in self.arrivals
        self.copy(0, name, dst, dst, device).wait_recv()

    def finish(self):
        for _, one, when in self.free:
            self.wait(one, when)


ARRIVALS = 110


def kernel(tokens, gate, up, down, out, tok, wgu, wd, part, pair, zs, zr, hid, mix, s1, r1, t1, t1s, r2, t2, z3, local_sem, send_sem, recv_sem):
    dp, tensor = lax.axis_index("dp"), lax.axis_index("tensor")
    x, y, zh = dp // 8, (dp // 2) % 4, dp % 2
    zl, core = tensor // 2, tensor % 2
    pos = jnp.where(core == 0, zl, 3 - zl)
    step = jnp.where(core == 0, 1, -1)

    def plane(dx, dy):
        return ((((x + dx + 4) % 4) * 4 + (y + dy + 4) % 4) * 2 + zh, tensor)

    across = ((x * 4 + y) * 2 + 1 - zh, tensor)
    mate = (dp, zl * 2 + 1 - core)
    ahead = (dp, (zl + step) * 2 + core)
    behind = (dp, (zl - step) * 2 + core)

    def columns(j):
        return pl.ds(256 * SPLIT[j][0], 256 * (SPLIT[j][1] - SPLIT[j][0]))

    def units(j):
        return pl.ds(128 * SPLIT[j][0], 128 * (SPLIT[j][1] - SPLIT[j][0]))

    def own(k):
        return 2 * k + (x + y) % 2, y // 2, y % 2, x // 2

    barrier = pltpu.get_barrier_semaphore()

    def greet(device):
        pl.semaphore_signal(barrier, inc=1, device_id=device, device_id_type=pl.DeviceIdType.MESH)

    mine = [
        pltpu.make_async_copy(tokens.at[pl.ds(16 * h, 16)], tok.at[own(OWN[h])], local_sem.at[h])
        for h in range(2)
    ]
    for one in mine:
        one.start()
    for dx, dy in ((1, 0), (-1, 0), (2, 0), (0, 1), (0, -1), (0, 2)):
        greet(plane(dx, dy))
    greet(across)
    greet(mate)
    pl.when(pos < 3)(lambda: greet(ahead))
    pl.when(pos > 0)(lambda: greet(behind))
    for j in range(PIECES):
        for n in range(*SPLIT[j]):
            for g, ref in enumerate((gate, up)):
                pltpu.make_async_copy(
                    ref.at[:, pl.ds(128 * n, 128)],
                    wgu.at[:, pl.ds(256 * n + 128 * g, 128)],
                    local_sem.at[2 + j],
                ).start()
    weights = [
        pltpu.make_async_copy(wgu.at[:, columns(j)], wgu.at[:, columns(j)], local_sem.at[2 + j])
        for j in range(PIECES)
    ]
    weights.append(pltpu.make_async_copy(down, wd, local_sem.at[2 + PIECES]))
    weights[-1].start()
    unread = set(range(PIECES + 1))

    def weight(j):
        if j in unread:
            unread.remove(j)
            weights[j].wait()

    pl.semaphore_wait(barrier, 8 + jnp.where(pos < 3, 1, 0) + jnp.where(pos > 0, 1, 0))

    net = Net(send_sem, recv_sem)

    def light(s, d):
        return plane(d, 0) if s == 0 else plane(0, d)

    def heavy(s, d):
        return plane(0, d) if s == 0 else plane(d, 0)

    here = ((y, x), (x, y))

    def line_of(ref, q, s, a):
        cols = pl.ds(1024 * s, 1024)
        if s == 0:
            return ref.at[q, a // 2, a % 2, :, :, cols]
        return ref.at[q, :, (q + a) % 2, a // 2, :, cols]

    def tokens_out(h):
        mine[h].wait()
        net.start(("z", h), tok.at[own(OWN[h])], tok.at[own(OTHER[h])], across)

    def tokens_light(k):
        if k in OTHER:
            net.arrived(("z", HALF_OF[k]), tok.at[own(k)], across)
        for s in range(2):
            block = tok.at[(*own(k), slice(None), pl.ds(1024 * s, 1024))]
            for d in (1, -1, 2):
                net.start(("light", k, s), block, block, light(s, d))

    came = set()

    def tokens_heavy(q, s):
        if (q // 2, s) not in came:
            came.add((q // 2, s))
            three = tok.at[pl.ds(0, 3), 0, 0, 0, :, pl.ds(0, 1024)]
            net.arrived(("light", q // 2, s), three, light(s, 1))
        line = line_of(tok, q, s, here[s][0])
        for d in (1, -1, 2):
            net.start(("heavy", q, s), line, line, heavy(s, d))

    def tokens_in(q):
        for s in range(2):
            net.arrived(("heavy", q, s), tok.at[pl.ds(0, 3), :, 0, 0, :, pl.ds(0, 1024)], heavy(s, 1))

    def multiply(k, j):
        weight(j)

        @pl.loop(*SPLIT[j])
        def _(n):
            cols = pl.ds(pl.multiple_of(n * 256, 256), 256)
            value = jnp.dot(tok[k].reshape(128, 2048), wgu[:, cols], preferred_element_type=F32)
            part[k, :, :, cols] = value.reshape(2, 64, 256)

        net.start(("pair", k, j), part.at[k, 1 - core, :, columns(j)], pair.at[k, :, columns(j)], mate)

    def total(k, j, rows, *more):
        cols = columns(j)
        value = part[k, core, rows, cols] + pair[k, rows, cols]
        for ref in more:
            value = value + ref[k, rows, cols].astype(F32)
        return value

    held = {}

    def end(k, j):
        return 2 if MEET[k][j] else 3

    def line_copy(k, j, up):
        src = zs.at[k, :, columns(j)]
        if up:
            return net.copy(held["line", k, j], ("line", k, j), src, zr.at[k, :, columns(j)], ahead)
        return net.copy(held["line", k, j], ("line", k, j), src, src, behind)

    def pass_on(k, j, up, *more):
        @pl.loop(0, 4)
        def _(r):
            rows = pl.ds(pl.multiple_of(r * 16, 16), 16)
            zs[k, rows, columns(j)] = total(k, j, rows, *more).astype(BF16)

        line_copy(k, j, up).start()

    def hidden_copy(k, j, name):
        block = hid.at[k, core, :, units(j)]
        arrival = ("share", k) if name == "share" else ("back", k, j)
        device = {"share": mate, "back": behind, "onward": ahead}[name]
        return net.copy(held[name, k, j], arrival, block, block, device)

    def hidden_out(k, j, *names):
        for name in names:
            hidden_copy(k, j, name).start()

    def activate(k, j, *more):
        @pl.loop(0, 4)
        def _(r):
            rows = pl.ds(pl.multiple_of(r * 16, 16), 16)
            value = total(k, j, rows, *more)
            for n in range(SPLIT[j][1] - SPLIT[j][0]):
                g, u = value[:, 256 * n : 256 * n + 128], value[:, 256 * n + 128 : 256 * n + 256]
                unit = 128 * (SPLIT[j][0] + n)
                hid[k, core, rows, unit : unit + 128] = (g / (1.0 + jnp.exp(-g)) * u).astype(BF16)

    def line(k, j, p):
        if p == 0:
            held["line", k, j] = net.take()
            net.arrived(("pair", k, j), pair.at[k, :, columns(j)], mate)
        if p == end(k, j):
            for name in ("back", "share") + (("onward",) if MEET[k][j] else ()):
                held[name, k, j] = net.take()

        def go():
            if p == 0:
                pass_on(k, j, True)
                return
            if p == end(k, j) and MEET[k][j]:
                net.arrived(("line", k, j), zr.at[pl.ds(0, 2), :, columns(j)], behind)
            else:
                net.arrived(("line", k, j), zr.at[k, :, columns(j)], behind)
            if p < end(k, j):
                pass_on(k, j, True, zr)
            elif MEET[k][j]:
                activate(k, j, zr, zs)
                hidden_out(k, j, "back", "onward", "share")
            else:
                activate(k, j, zr)
                hidden_out(k, j, "back", "share")

        pl.when(pos == p)(go)
        if p == 0 and MEET[k][j]:
            pl.when(pos == 3)(lambda: pass_on(k, j, False))
        if p == end(k, j) - 1:
            net.give(held["line", k, j], line_copy(k, j, True), pos != end(k, j))

    backs = {}

    def back(k, j, p):
        def go():
            net.arrived(("back", k, j), hid.at[k, core, :, units(j)], ahead if p < end(k, j) else behind)
            hidden_out(k, j, *(("back",) if p and p < end(k, j) else ()), "share")

        pl.when(pos == p)(go)
        backs[k, j] = backs.get((k, j), 0) + 1
        if backs[k, j] == 3:
            senders = (pos == 1) | (pos == 2) if MEET[k][j] else pos > 0
            net.give(held["back", k, j], hidden_copy(k, j, "back"), senders)
            net.give(held["share", k, j], hidden_copy(k, j, "share"))
            if MEET[k][j]:
                net.give(held["onward", k, j], hidden_copy(k, j, "onward"), pos == 2)

    def project(q, s):
        if s == 0:
            weight(PIECES)
            net.arrived(("share", q), hid.at[q, 1 - core], mate)

        @pl.loop(4 * s, 4 * s + 4)
        def _(n):
            cols = pl.ds(pl.multiple_of(n * 256, 256), 256)
            value = jnp.dot(hid[q].reshape(128, 896), wd[:, cols], preferred_element_type=F32)
            mix[q, :, :, :, :, cols] = value.reshape(2, 2, 2, 16, 256)

        a, b = here[s]
        for i, d in enumerate((1, -1, 2)):
            s1[q, s, i] = line_of(mix, q, s, (a + d + 4) % 4)[...].astype(BF16)
            net.start(("last", q, s), s1.at[q, s, i], r1.at[q, s, i], heavy(s, d))

    def scatter_light(k, s):
        a, b = here[s]
        for p in range(2):
            q = 2 * k + p
            net.arrived(("last", q, s), r1.at[q, s], heavy(s, 1))
            value = line_of(mix, q, s, a)[...]
            for i in range(3):
                value = value + r1[q, s, i].astype(F32)
            for i in range(2):
                t1[k, s, 2 * i + (p + a) % 2] = value[i]
                t1s[k, s, 2 * i + (p + a) % 2] = value[i].astype(BF16)
        for i, d in enumerate((1, -1, 2)):
            net.start(("second", k, s), t1s.at[k, s, (b + d + 4) % 4], r2.at[k, s, i], light(s, d))

    def scatter_across(k, s):
        a, b = here[s]
        net.arrived(("second", k, s), r2.at[k, s], light(s, 1))
        value = t1[k, s, b]
        for i in range(3):
            value = value + r2[k, s, i].astype(F32)
        h = HALF_OF[k]
        if k in OTHER:
            t2[h, s] = value.astype(BF16)
            net.start(("third", h, s), t2.at[h, s], z3.at[h, s], across)
        else:
            net.arrived(("third", h, s), z3.at[h, s], across)
            out[16 * h : 16 * h + 16, 1024 * s : 1024 * s + 1024] = (value + z3[h, s].astype(F32)).astype(BF16)

    STEPS = (
        tokens_out, tokens_light, tokens_heavy, None, tokens_in, multiply,
        line, back, project, None, scatter_light, scatter_across,
    )
    for number, *args in ORDER:
        STEPS[number](*args)
    net.finish()


def on_device(tokens, gate_weight, up_weight, down_weight):
    hbm = pl.BlockSpec(memory_space=pl.ANY)
    n, g = CHUNKS, GROUPS
    return pl.pallas_call(
        kernel,
        out_shape=pltpu.VMEM((32, 2048), BF16),
        in_specs=[hbm] * 4,
        out_specs=pl.BlockSpec(memory_space=pltpu.VMEM),
        scratch_shapes=[
            pltpu.VMEM((n, 2, 2, 2, 16, 2048), BF16),
            pltpu.VMEM((2048, 1792), BF16),
            pltpu.VMEM((896, 2048), BF16),
            pltpu.VMEM((n, 2, 64, 1792), F32),
            pltpu.VMEM((n, 64, 1792), F32),
            pltpu.VMEM((n, 64, 1792), BF16),
            pltpu.VMEM((n, 64, 1792), BF16),
            pltpu.VMEM((n, 2, 64, 896), BF16),
            pltpu.VMEM((n, 2, 2, 2, 16, 2048), F32),
            pltpu.VMEM((n, 2, 3, 2, 16, 1024), BF16),
            pltpu.VMEM((n, 2, 3, 2, 16, 1024), BF16),
            pltpu.VMEM((g, 2, 4, 16, 1024), F32),
            pltpu.VMEM((g, 2, 4, 16, 1024), BF16),
            pltpu.VMEM((g, 2, 3, 16, 1024), BF16),
            pltpu.VMEM((2, 2, 16, 1024), BF16),
            pltpu.VMEM((2, 2, 16, 1024), BF16),
            pltpu.SemaphoreType.DMA((3 + PIECES,)),
            pltpu.SemaphoreType.DMA((POOL,)),
            pltpu.SemaphoreType.DMA((ARRIVALS,)),
        ],
        compiler_params=pltpu.CompilerParams(
            collective_id=0, has_side_effects=True, vmem_limit_bytes=60 * 2**20
        ),
        name="panel",
    )(tokens, gate_weight, up_weight, down_weight)


def solution(mesh):
    return jax.shard_map(
        on_device,
        mesh=mesh,
        in_specs=(P("dp", "tensor"), P("tensor", "dp"), P("tensor", "dp"), P("dp", "tensor")),
        out_specs=P("dp", "tensor"),
        check_vma=False,
    )
```

```python
import jax
import jax.numpy as jnp
from jax import lax
from jax.experimental import pallas as pl
from jax.experimental.pallas import tpu as pltpu
from jax.sharding import PartitionSpec as P

F32, BF16 = jnp.float32, jnp.bfloat16
GROUPS = 4
OWN, OTHER, HALF_OF = (0, 3), (1, 2), (0, 0, 1, 1)
CHUNKS = 8
SPLIT = (((0, 4), (4, 7)), ((0, 1), (1, 4), (4, 7)), ((0, 4), (4, 7)), ((0, 4), (4, 7)), ((0, 4), (4, 7)), ((0, 4), (4, 7)), ((0, 4), (4, 7)), ((0, 4), (4, 7)))
EARLY = (0, 7)
MEET = ((1, 1), (1, 1, 1), (1, 1), (1, 1), (1, 1), (1, 1), (1, 1), (1, 1))
POOL = 40
CUTS = sorted({edge for pieces in SPLIT for piece in pieces for edge in piece})
PARTS = tuple(zip(CUTS, CUTS[1:]))

ORDER = (
    (0, 1), (0, 0), (1, 0), (1, 3), (2, 1, 0), (2, 1, 1), (1, 2), (1, 1), (4, 1), (5, 1, 0), (2, 5, 1),
    (2, 5, 0), (5, 1, 2), (2, 4, 1), (2, 4, 0), (6, 1, 0, 0), (2, 3, 1), (5, 1, 1), (2, 3, 0), (2, 2, 1),
    (6, 1, 0, 1), (6, 1, 2, 0), (2, 2, 0), (4, 5), (5, 5, 1), (6, 1, 1, 0), (6, 1, 2, 1), (5, 5, 0),
    (6, 5, 1, 0), (2, 6, 0), (2, 6, 1), (2, 7, 1), (2, 7, 0), (2, 0, 0), (4, 4), (5, 4, 1), (6, 5, 0, 0),
    (6, 1, 1, 1), (6, 5, 1, 1), (5, 4, 0), (2, 0, 1), (6, 5, 0, 1), (6, 1, 2, 2), (6, 1, 0, 2), (4, 3),
    (5, 3, 0), (6, 4, 1, 0), (5, 3, 1), (6, 4, 1, 1), (4, 2), (6, 4, 0, 0), (7, 1, 2, 3), (5, 2, 0),
    (6, 5, 1, 2), (6, 1, 1, 2), (5, 2, 1), (4, 6), (6, 3, 1, 0), (6, 3, 0, 0), (6, 4, 0, 1), (4, 7), (5, 6, 0),
    (6, 5, 0, 2), (6, 3, 1, 1), (5, 7, 0), (6, 2, 0, 0), (6, 4, 1, 2), (5, 6, 1), (7, 1, 1, 3), (7, 5, 1, 3),
    (6, 3, 0, 1), (6, 2, 1, 0), (7, 1, 2, 1), (4, 0), (7, 1, 0, 3), (5, 0, 0), (6, 4, 0, 2), (7, 5, 0, 1),
    (5, 7, 1), (7, 5, 1, 1), (7, 5, 0, 3), (7, 4, 1, 3), (7, 4, 1, 1), (6, 3, 1, 2), (7, 1, 1, 1),
    (7, 3, 1, 3), (7, 4, 0, 3), (6, 2, 0, 1), (6, 7, 0, 0), (5, 0, 1), (6, 3, 0, 2), (6, 6, 0, 0),
    (7, 5, 0, 0), (6, 6, 1, 0), (6, 7, 1, 0), (6, 2, 1, 1), (7, 5, 1, 0), (8, 5, 0), (7, 4, 0, 1),
    (7, 4, 1, 0), (6, 2, 0, 2), (8, 5, 1), (6, 7, 0, 1), (6, 0, 0, 0), (7, 3, 1, 1), (7, 4, 0, 0),
    (7, 1, 0, 1), (6, 0, 1, 0), (7, 3, 0, 3), (7, 1, 1, 0), (6, 2, 1, 2), (7, 3, 0, 1), (8, 4, 0), (8, 4, 1),
    (7, 3, 1, 0), (7, 3, 0, 0), (6, 6, 0, 1), (7, 2, 0, 1), (7, 2, 1, 3), (7, 1, 2, 0), (6, 7, 0, 2),
    (7, 2, 0, 3), (6, 6, 1, 1), (8, 3, 0), (7, 2, 1, 1), (8, 3, 1), (6, 6, 0, 2), (6, 7, 1, 1), (7, 2, 0, 0),
    (6, 6, 1, 2), (7, 7, 0, 3), (7, 2, 1, 0), (8, 2, 0), (7, 6, 1, 3), (10, 2, 0), (7, 1, 0, 0), (6, 0, 0, 1),
    (10, 2, 1), (7, 7, 0, 1), (6, 7, 1, 2), (6, 0, 1, 1), (8, 2, 1), (7, 6, 0, 1), (7, 6, 0, 3), (8, 1, 0),
    (7, 6, 1, 1), (6, 0, 0, 2), (8, 1, 1), (7, 7, 0, 0), (6, 0, 1, 2), (7, 6, 0, 0), (7, 0, 0, 3), (10, 1, 0),
    (7, 7, 1, 3), (7, 6, 1, 0), (7, 7, 1, 1), (8, 6, 0), (8, 6, 1), (7, 0, 0, 1), (10, 1, 1), (7, 7, 1, 0),
    (12, 7, 0), (7, 0, 1, 1), (7, 0, 1, 3), (11, 2, 1), (12, 7, 1), (8, 7, 0), (7, 0, 0, 0), (8, 7, 1),
    (12, 0, 0), (11, 2, 0), (7, 0, 1, 0), (12, 0, 1), (8, 0, 0), (8, 0, 1), (11, 1, 0), (11, 1, 1), (10, 3, 0),
    (10, 3, 1), (10, 0, 0), (10, 0, 1), (11, 3, 0), (11, 3, 1), (11, 0, 0), (11, 0, 1),
)


class Net:
    def __init__(self, send_sem, recv_sem):
        self.send_sem, self.recv_sem = send_sem, recv_sem
        self.arrivals, self.free, self.slots = {}, [], 0

    def take(self):
        if self.slots < POOL:
            self.slots += 1
            return self.slots - 1
        slot, one, when = self.free.pop(0)
        self.wait(one, when)
        return slot

    def give(self, slot, one, when=None):
        self.free.append((slot, one, when))

    def wait(self, one, when):
        if when is None:
            one.wait_send()
        else:
            pl.when(when)(one.wait_send)

    def copy(self, slot, name, src, dst, device):
        number = self.arrivals.setdefault(name, len(self.arrivals))
        return pltpu.make_async_remote_copy(
            src_ref=src,
            dst_ref=dst,
            send_sem=self.send_sem.at[slot],
            recv_sem=self.recv_sem.at[number],
            device_id=device,
            device_id_type=pl.DeviceIdType.MESH,
        )

    def start(self, name, src, dst, device):
        slot = self.take()
        one = self.copy(slot, name, src, dst, device)
        one.start()
        self.give(slot, one)

    def arrived(self, name, dst, device):
        assert name in self.arrivals
        self.copy(0, name, dst, dst, device).wait_recv()

    def finish(self):
        for _, one, when in self.free:
            self.wait(one, when)


ARRIVALS = 115


def kernel(tokens, gate, up, down, out, tok, wgu, wd, part, pair, zs, zr, hid, mix, s1, r1, t1, t1s, r2, t2, z3, local_sem, send_sem, recv_sem):
    dp, tensor = lax.axis_index("dp"), lax.axis_index("tensor")
    x, y, zh = dp // 8, (dp // 2) % 4, dp % 2
    zl, core = tensor // 2, tensor % 2
    pos = jnp.where(core == 0, zl, 3 - zl)
    step = jnp.where(core == 0, 1, -1)

    def plane(dx, dy):
        return ((((x + dx + 4) % 4) * 4 + (y + dy + 4) % 4) * 2 + zh, tensor)

    across = ((x * 4 + y) * 2 + 1 - zh, tensor)
    mate = (dp, zl * 2 + 1 - core)
    ahead = (dp, (zl + step) * 2 + core)
    behind = (dp, (zl - step) * 2 + core)

    def tiles(first, last, width):
        return pl.ds(width * first, width * (last - first))

    def columns(q, j):
        return tiles(*SPLIT[q][j], 256)

    def units(q, j):
        return tiles(*SPLIT[q][j], 128)

    def own(k):
        return 2 * k + (x + y) % 2, y // 2, y % 2, x // 2

    barrier = pltpu.get_barrier_semaphore()

    def greet(device):
        pl.semaphore_signal(barrier, inc=1, device_id=device, device_id_type=pl.DeviceIdType.MESH)

    mine = [
        pltpu.make_async_copy(tokens.at[pl.ds(16 * h, 16)], tok.at[own(OWN[h])], local_sem.at[h])
        for h in range(2)
    ]
    for one in mine:
        one.start()
    for dx, dy in ((1, 0), (-1, 0), (2, 0), (0, 1), (0, -1), (0, 2)):
        greet(plane(dx, dy))
    greet(across)
    greet(mate)
    pl.when(pos < 3)(lambda: greet(ahead))
    pl.when(pos > 0)(lambda: greet(behind))
    weights = []

    def load_weights():
        for i, part_of in enumerate(PARTS):
            for n in range(*part_of):
                for g, ref in enumerate((gate, up)):
                    pltpu.make_async_copy(
                        ref.at[:, pl.ds(128 * n, 128)],
                        wgu.at[:, pl.ds(256 * n + 128 * g, 128)],
                        local_sem.at[2 + i],
                    ).start()
            block = wgu.at[:, tiles(*part_of, 256)]
            weights.append(pltpu.make_async_copy(block, block, local_sem.at[2 + i]))
        weights.append(pltpu.make_async_copy(down, wd, local_sem.at[2 + len(PARTS)]))
        weights[-1].start()

    load_weights()
    unread = set(range(len(weights)))

    def weight(i):
        if i in unread:
            unread.remove(i)
            weights[i].wait()

    pl.semaphore_wait(barrier, 8 + jnp.where(pos < 3, 1, 0) + jnp.where(pos > 0, 1, 0))

    net = Net(send_sem, recv_sem)

    def light(s, d):
        return plane(d, 0) if s == 0 else plane(0, d)

    def heavy(s, d):
        return plane(0, d) if s == 0 else plane(d, 0)

    here = ((y, x), (x, y))

    def line_of(ref, q, s, a):
        cols = pl.ds(1024 * s, 1024)
        if s == 0:
            return ref.at[q, a // 2, a % 2, :, :, cols]
        return ref.at[q, :, (q + a) % 2, a // 2, :, cols]

    def tokens_out(h):
        mine[h].wait()
        net.start(("z", h), tok.at[own(OWN[h])], tok.at[own(OTHER[h])], across)

    def tokens_light(k):
        if k in OTHER:
            net.arrived(("z", HALF_OF[k]), tok.at[own(k)], across)
        for s in range(2):
            block = tok.at[(*own(k), slice(None), pl.ds(1024 * s, 1024))]
            for d in (1, -1, 2):
                net.start(("light", k, s), block, block, light(s, d))

    came = set()

    def tokens_heavy(q, s):
        if (q // 2, s) not in came:
            came.add((q // 2, s))
            three = tok.at[pl.ds(0, 3), 0, 0, 0, :, pl.ds(0, 1024)]
            net.arrived(("light", q // 2, s), three, light(s, 1))
        line = line_of(tok, q, s, here[s][0])
        for d in (1, -1, 2):
            net.start(("heavy", q, s), line, line, heavy(s, d))

    def tokens_in(q):
        for s in range(2):
            net.arrived(("heavy", q, s), tok.at[pl.ds(0, 3), :, 0, 0, :, pl.ds(0, 1024)], heavy(s, 1))

    def multiply(k, j):
        for i, (first, _) in enumerate(PARTS):
            if SPLIT[k][j][0] <= first < SPLIT[k][j][1]:
                weight(i)

        @pl.loop(*SPLIT[k][j])
        def _(n):
            cols = pl.ds(pl.multiple_of(n * 256, 256), 256)
            value = jnp.dot(tok[k].reshape(128, 2048), wgu[:, cols], preferred_element_type=F32)
            part[k, :, :, cols] = value.reshape(2, 64, 256)

        net.start(("pair", k, j), part.at[k, 1 - core, :, columns(k, j)], pair.at[k, :, columns(k, j)], mate)

    def total(k, j, rows, *more):
        cols = columns(k, j)
        value = part[k, core, rows, cols] + pair[k, rows, cols]
        for ref in more:
            value = value + ref[k, rows, cols].astype(F32)
        return value

    held = {}

    def end(k, j):
        return 2 if MEET[k][j] else 3

    def line_copy(k, j, up):
        src = zs.at[k, :, columns(k, j)]
        if up:
            return net.copy(held["line", k, j], ("line", k, j), src, zr.at[k, :, columns(k, j)], ahead)
        return net.copy(held["line", k, j], ("line", k, j), src, src, behind)

    def pass_on(k, j, up, *more):
        @pl.loop(0, 4)
        def _(r):
            rows = pl.ds(pl.multiple_of(r * 16, 16), 16)
            zs[k, rows, columns(k, j)] = total(k, j, rows, *more).astype(BF16)

        line_copy(k, j, up).start()

    def hidden_copy(k, j, name):
        block = hid.at[k, core, :, units(k, j)]
        final = k in EARLY and j == len(SPLIT[k]) - 1
        arrival = ("share", k, final) if name == "share" else ("back", k, j)
        device = {"share": mate, "back": behind, "onward": ahead}[name]
        return net.copy(held[name, k, j], arrival, block, block, device)

    def hidden_out(k, j, *names):
        for name in names:
            hidden_copy(k, j, name).start()

    def activate(k, j, *more):
        @pl.loop(0, 4)
        def _(r):
            rows = pl.ds(pl.multiple_of(r * 16, 16), 16)
            value = total(k, j, rows, *more)
            for n in range(SPLIT[k][j][1] - SPLIT[k][j][0]):
                g, u = value[:, 256 * n : 256 * n + 128], value[:, 256 * n + 128 : 256 * n + 256]
                unit = 128 * (SPLIT[k][j][0] + n)
                hid[k, core, rows, unit : unit + 128] = (g / (1.0 + jnp.exp(-g)) * u).astype(BF16)

    def line(k, j, p):
        if p == 0:
            held["line", k, j] = net.take()
            net.arrived(("pair", k, j), pair.at[k, :, columns(k, j)], mate)
        if p == end(k, j):
            for name in ("back", "share") + (("onward",) if MEET[k][j] else ()):
                held[name, k, j] = net.take()

        def go():
            if p == 0:
                pass_on(k, j, True)
                return
            if p == end(k, j) and MEET[k][j]:
                net.arrived(("line", k, j), zr.at[pl.ds(0, 2), :, columns(k, j)], behind)
            else:
                net.arrived(("line", k, j), zr.at[k, :, columns(k, j)], behind)
            if p < end(k, j):
                pass_on(k, j, True, zr)
            elif MEET[k][j]:
                activate(k, j, zr, zs)
                hidden_out(k, j, "back", "onward", "share")
            else:
                activate(k, j, zr)
                hidden_out(k, j, "back", "share")

        pl.when(pos == p)(go)
        if p == 0 and MEET[k][j]:
            pl.when(pos == 3)(lambda: pass_on(k, j, False))
        if p == end(k, j) - 1:
            net.give(held["line", k, j], line_copy(k, j, True), pos != end(k, j))

    backs = {}

    def back(k, j, p):
        def go():
            net.arrived(("back", k, j), hid.at[k, core, :, units(k, j)], ahead if p < end(k, j) else behind)
            hidden_out(k, j, *(("back",) if p and p < end(k, j) else ()), "share")

        pl.when(pos == p)(go)
        backs[k, j] = backs.get((k, j), 0) + 1
        if backs[k, j] == 3:
            senders = (pos == 1) | (pos == 2) if MEET[k][j] else pos > 0
            net.give(held["back", k, j], hidden_copy(k, j, "back"), senders)
            net.give(held["share", k, j], hidden_copy(k, j, "share"))
            if MEET[k][j]:
                net.give(held["onward", k, j], hidden_copy(k, j, "onward"), pos == 2)

    def down_product(q, s, first, last, more):
        if s == 0:
            weight(len(PARTS))
            net.arrived(("share", q, more), hid.at[q, 1 - core, :, pl.ds(first, last - first)], mate)

        @pl.loop(4 * s, 4 * s + 4)
        def _(n):
            cols = pl.ds(pl.multiple_of(n * 256, 256), 256)
            value = jnp.dot(
                hid[q, :, :, first:last].reshape(128, last - first), wd[first:last, cols], preferred_element_type=F32
            ).reshape(2, 2, 2, 16, 256)
            mix[q, :, :, :, :, cols] = mix[q, :, :, :, :, cols] + value if more else value

    def begin(q, s):
        down_product(q, s, 0, 128 * SPLIT[q][-1][0], False)

    def project(q, s):
        early = q in EARLY
        down_product(q, s, 128 * SPLIT[q][-1][0] if early else 0, 896, early)
        a, b = here[s]
        for i, d in enumerate((1, -1, 2)):
            s1[q, s, i] = line_of(mix, q, s, (a + d + 4) % 4)[...].astype(BF16)
            net.start(("last", q, s), s1.at[q, s, i], r1.at[q, s, i], heavy(s, d))

    def scatter_light(k, s):
        a, b = here[s]
        for p in range(2):
            q = 2 * k + p
            net.arrived(("last", q, s), r1.at[q, s], heavy(s, 1))
            value = line_of(mix, q, s, a)[...]
            for i in range(3):
                value = value + r1[q, s, i].astype(F32)
            for i in range(2):
                t1[k, s, 2 * i + (p + a) % 2] = value[i]
                t1s[k, s, 2 * i + (p + a) % 2] = value[i].astype(BF16)
        for i, d in enumerate((1, -1, 2)):
            net.start(("second", k, s), t1s.at[k, s, (b + d + 4) % 4], r2.at[k, s, i], light(s, d))

    def scatter_across(k, s):
        a, b = here[s]
        net.arrived(("second", k, s), r2.at[k, s], light(s, 1))
        value = t1[k, s, b]
        for i in range(3):
            value = value + r2[k, s, i].astype(F32)
        h = HALF_OF[k]
        if k in OTHER:
            t2[h, s] = value.astype(BF16)
            net.start(("third", h, s), t2.at[h, s], z3.at[h, s], across)
        else:
            net.arrived(("third", h, s), z3.at[h, s], across)
            out[16 * h : 16 * h + 16, 1024 * s : 1024 * s + 1024] = (value + z3[h, s].astype(F32)).astype(BF16)

    STEPS = (
        tokens_out, tokens_light, tokens_heavy, None, tokens_in, multiply,
        line, back, project, None, scatter_light, scatter_across, begin,
    )
    for number, *args in ORDER:
        STEPS[number](*args)
    net.finish()


def on_device(tokens, gate_weight, up_weight, down_weight):
    hbm = pl.BlockSpec(memory_space=pl.ANY)
    n, g = CHUNKS, GROUPS
    return pl.pallas_call(
        kernel,
        out_shape=pltpu.VMEM((32, 2048), BF16),
        in_specs=[hbm] * 4,
        out_specs=pl.BlockSpec(memory_space=pltpu.VMEM),
        scratch_shapes=[
            pltpu.VMEM((n, 2, 2, 2, 16, 2048), BF16),
            pltpu.VMEM((2048, 1792), BF16),
            pltpu.VMEM((896, 2048), BF16),
            pltpu.VMEM((n, 2, 64, 1792), F32),
            pltpu.VMEM((n, 64, 1792), F32),
            pltpu.VMEM((n, 64, 1792), BF16),
            pltpu.VMEM((n, 64, 1792), BF16),
            pltpu.VMEM((n, 2, 64, 896), BF16),
            pltpu.VMEM((n, 2, 2, 2, 16, 2048), F32),
            pltpu.VMEM((n, 2, 3, 2, 16, 1024), BF16),
            pltpu.VMEM((n, 2, 3, 2, 16, 1024), BF16),
            pltpu.VMEM((g, 2, 4, 16, 1024), F32),
            pltpu.VMEM((g, 2, 4, 16, 1024), BF16),
            pltpu.VMEM((g, 2, 3, 16, 1024), BF16),
            pltpu.VMEM((2, 2, 16, 1024), BF16),
            pltpu.VMEM((2, 2, 16, 1024), BF16),
            pltpu.SemaphoreType.DMA((3 + len(PARTS),)),
            pltpu.SemaphoreType.DMA((POOL,)),
            pltpu.SemaphoreType.DMA((ARRIVALS,)),
        ],
        compiler_params=pltpu.CompilerParams(
            collective_id=0, has_side_effects=True, vmem_limit_bytes=60 * 2**20
        ),
        name="panel",
    )(tokens, gate_weight, up_weight, down_weight)


def solution(mesh):
    return jax.shard_map(
        on_device,
        mesh=mesh,
        in_specs=(P("dp", "tensor"), P("tensor", "dp"), P("tensor", "dp"), P("dp", "tensor")),
        out_specs=P("dp", "tensor"),
        check_vma=False,
    )
```

```python
import jax
import jax.numpy as jnp
from jax import lax
from jax.experimental import pallas as pl
from jax.experimental.pallas import tpu as pltpu
from jax.sharding import PartitionSpec as P

F32, BF16 = jnp.float32, jnp.bfloat16
GROUPS = 4
OWN, OTHER, HALF_OF = (0, 3), (1, 2), (0, 0, 1, 1)
CHUNKS = 8
SPLIT = (((0, 4), (4, 7)), ((0, 1), (1, 4), (4, 7)), ((0, 4), (4, 7)), ((0, 4), (4, 7)), ((0, 4), (4, 7)), ((0, 4), (4, 7)), ((0, 4), (4, 7)), ((0, 4), (4, 7)))
EARLY = (0, 7)
MEET = ((1, 1), (1, 1, 1), (1, 1), (1, 1), (1, 1), (1, 1), (1, 1), (1, 1))
POOL = 40
CUTS = sorted({edge for pieces in SPLIT for piece in pieces for edge in piece})
PARTS = tuple(zip(CUTS, CUTS[1:]))

ORDER = (
    (0, 1), (1, 0), (1, 3), (2, 1, 0), (2, 1, 1), (0, 0), (1, 2), (4, 1), (5, 1, 0), (2, 5, 1),
    (2, 5, 0), (5, 1, 2), (1, 1), (2, 4, 1), (2, 4, 0), (6, 1, 0, 0), (2, 3, 1), (5, 1, 1), (2, 3, 0), (2, 2, 1),
    (6, 1, 0, 1), (6, 1, 2, 0), (2, 2, 0), (4, 5), (5, 5, 1), (6, 1, 1, 0), (6, 1, 2, 1), (5, 5, 0),
    (6, 5, 1, 0), (2, 6, 0), (2, 6, 1), (2, 7, 1), (2, 7, 0), (2, 0, 0), (4, 4), (5, 4, 1), (6, 5, 0, 0),
    (6, 1, 1, 1), (6, 5, 1, 1), (5, 4, 0), (2, 0, 1), (6, 5, 0, 1), (6, 1, 2, 2), (6, 1, 0, 2), (4, 3),
    (5, 3, 0), (6, 4, 1, 0), (5, 3, 1), (6, 4, 1, 1), (4, 2), (6, 4, 0, 0), (7, 1, 2, 3), (5, 2, 0),
    (6, 5, 1, 2), (6, 1, 1, 2), (5, 2, 1), (4, 6), (6, 3, 1, 0), (6, 3, 0, 0), (6, 4, 0, 1), (4, 7), (5, 6, 0),
    (6, 5, 0, 2), (6, 3, 1, 1), (5, 7, 0), (6, 2, 0, 0), (6, 4, 1, 2), (5, 6, 1), (7, 1, 1, 3), (7, 5, 1, 3),
    (6, 3, 0, 1), (6, 2, 1, 0), (7, 1, 2, 1), (4, 0), (7, 1, 0, 3), (5, 0, 0), (6, 4, 0, 2), (7, 5, 0, 1),
    (5, 7, 1), (7, 5, 1, 1), (7, 5, 0, 3), (7, 4, 1, 3), (7, 4, 1, 1), (6, 3, 1, 2), (7, 1, 1, 1),
    (7, 3, 1, 3), (7, 4, 0, 3), (6, 2, 0, 1), (6, 7, 0, 0), (5, 0, 1), (6, 3, 0, 2), (6, 6, 0, 0),
    (7, 5, 0, 0), (6, 6, 1, 0), (6, 7, 1, 0), (6, 2, 1, 1), (7, 5, 1, 0), (8, 5, 0), (7, 4, 0, 1),
    (7, 4, 1, 0), (6, 2, 0, 2), (8, 5, 1), (6, 7, 0, 1), (6, 0, 0, 0), (7, 3, 1, 1), (7, 4, 0, 0),
    (7, 1, 0, 1), (6, 0, 1, 0), (7, 3, 0, 3), (7, 1, 1, 0), (6, 2, 1, 2), (7, 3, 0, 1), (8, 4, 0), (8, 4, 1),
    (7, 3, 1, 0), (7, 3, 0, 0), (6, 6, 0, 1), (7, 2, 0, 1), (7, 2, 1, 3), (7, 1, 2, 0), (6, 7, 0, 2),
    (7, 2, 0, 3), (6, 6, 1, 1), (8, 3, 0), (7, 2, 1, 1), (8, 3, 1), (6, 6, 0, 2), (6, 7, 1, 1), (7, 2, 0, 0),
    (6, 6, 1, 2), (7, 7, 0, 3), (7, 2, 1, 0), (8, 2, 0), (7, 6, 1, 3), (10, 2, 0), (7, 1, 0, 0), (6, 0, 0, 1),
    (10, 2, 1), (7, 7, 0, 1), (6, 7, 1, 2), (6, 0, 1, 1), (8, 2, 1), (7, 6, 0, 1), (7, 6, 0, 3), (8, 1, 0),
    (7, 6, 1, 1), (6, 0, 0, 2), (8, 1, 1), (7, 7, 0, 0), (6, 0, 1, 2), (7, 6, 0, 0), (7, 0, 0, 3), (10, 1, 0),
    (7, 7, 1, 3), (7, 6, 1, 0), (7, 7, 1, 1), (8, 6, 0), (8, 6, 1), (7, 0, 0, 1), (10, 1, 1), (7, 7, 1, 0),
    (12, 7, 0), (7, 0, 1, 1), (7, 0, 1, 3), (11, 2, 1), (12, 7, 1), (8, 7, 0), (7, 0, 0, 0), (8, 7, 1),
    (12, 0, 0), (11, 2, 0), (7, 0, 1, 0), (12, 0, 1), (8, 0, 0), (8, 0, 1), (11, 1, 0), (11, 1, 1), (10, 3, 0),
    (10, 3, 1), (10, 0, 0), (10, 0, 1), (11, 3, 0), (11, 3, 1), (11, 0, 0), (11, 0, 1),
)


class Net:
    def __init__(self, send_sem, recv_sem):
        self.send_sem, self.recv_sem = send_sem, recv_sem
        self.arrivals, self.free, self.slots = {}, [], 0

    def take(self):
        if self.slots < POOL:
            self.slots += 1
            return self.slots - 1
        slot, one, when = self.free.pop(0)
        self.wait(one, when)
        return slot

    def give(self, slot, one, when=None):
        self.free.append((slot, one, when))

    def wait(self, one, when):
        if when is None:
            one.wait_send()
        else:
            pl.when(when)(one.wait_send)

    def copy(self, slot, name, src, dst, device):
        number = self.arrivals.setdefault(name, len(self.arrivals))
        return pltpu.make_async_remote_copy(
            src_ref=src,
            dst_ref=dst,
            send_sem=self.send_sem.at[slot],
            recv_sem=self.recv_sem.at[number],
            device_id=device,
            device_id_type=pl.DeviceIdType.MESH,
        )

    def start(self, name, src, dst, device):
        slot = self.take()
        one = self.copy(slot, name, src, dst, device)
        one.start()
        self.give(slot, one)

    def arrived(self, name, dst, device):
        assert name in self.arrivals
        self.copy(0, name, dst, dst, device).wait_recv()

    def finish(self):
        for _, one, when in self.free:
            self.wait(one, when)


ARRIVALS = 115


def kernel(tokens, gate, up, down, out, tok, wgu, wd, part, pair, zs, zr, hid, mix, s1, r1, t1, t1s, r2, t2, z3, local_sem, send_sem, recv_sem):
    dp, tensor = lax.axis_index("dp"), lax.axis_index("tensor")
    x, y, zh = dp // 8, (dp // 2) % 4, dp % 2
    zl, core = tensor // 2, tensor % 2
    pos = jnp.where(core == 0, zl, 3 - zl)
    step = jnp.where(core == 0, 1, -1)

    def plane(dx, dy):
        return ((((x + dx + 4) % 4) * 4 + (y + dy + 4) % 4) * 2 + zh, tensor)

    across = ((x * 4 + y) * 2 + 1 - zh, tensor)
    mate = (dp, zl * 2 + 1 - core)
    ahead = (dp, (zl + step) * 2 + core)
    behind = (dp, (zl - step) * 2 + core)

    def tiles(first, last, width):
        return pl.ds(width * first, width * (last - first))

    def columns(q, j):
        return tiles(*SPLIT[q][j], 256)

    def units(q, j):
        return tiles(*SPLIT[q][j], 128)

    def own(k):
        return 2 * k + (x + y) % 2, y // 2, y % 2, x // 2

    barrier = pltpu.get_barrier_semaphore()

    def greet(device):
        pl.semaphore_signal(barrier, inc=1, device_id=device, device_id_type=pl.DeviceIdType.MESH)

    mine = [
        pltpu.make_async_copy(tokens.at[pl.ds(16 * h, 16)], tok.at[own(OWN[h])], local_sem.at[h])
        for h in range(2)
    ]
    for one in mine:
        one.start()
    for dx, dy in ((1, 0), (-1, 0), (2, 0), (0, 1), (0, -1), (0, 2)):
        greet(plane(dx, dy))
    greet(across)
    greet(mate)
    pl.when(pos < 3)(lambda: greet(ahead))
    pl.when(pos > 0)(lambda: greet(behind))
    weights = []

    def load_weights():
        for i, part_of in enumerate(PARTS):
            for n in range(*part_of):
                for g, ref in enumerate((gate, up)):
                    pltpu.make_async_copy(
                        ref.at[:, pl.ds(128 * n, 128)],
                        wgu.at[:, pl.ds(256 * n + 128 * g, 128)],
                        local_sem.at[2 + i],
                    ).start()
            block = wgu.at[:, tiles(*part_of, 256)]
            weights.append(pltpu.make_async_copy(block, block, local_sem.at[2 + i]))
        weights.append(pltpu.make_async_copy(down, wd, local_sem.at[2 + len(PARTS)]))
        weights[-1].start()

    load_weights()
    unread = set(range(len(weights)))

    def weight(i):
        if i in unread:
            unread.remove(i)
            weights[i].wait()

    pl.semaphore_wait(barrier, 8 + jnp.where(pos < 3, 1, 0) + jnp.where(pos > 0, 1, 0))

    net = Net(send_sem, recv_sem)

    def light(s, d):
        return plane(d, 0) if s == 0 else plane(0, d)

    def heavy(s, d):
        return plane(0, d) if s == 0 else plane(d, 0)

    here = ((y, x), (x, y))

    def line_of(ref, q, s, a):
        cols = pl.ds(1024 * s, 1024)
        if s == 0:
            return ref.at[q, a // 2, a % 2, :, :, cols]
        return ref.at[q, :, (q + a) % 2, a // 2, :, cols]

    unheld = {0, 1}

    def hold(h):
        if h in unheld:
            unheld.remove(h)
            mine[h].wait()

    def tokens_out(h):
        hold(h)
        net.start(("z", h), tok.at[own(OWN[h])], tok.at[own(OTHER[h])], across)

    def tokens_light(k):
        if k in OTHER:
            net.arrived(("z", HALF_OF[k]), tok.at[own(k)], across)
        else:
            hold(HALF_OF[k])
        for s in range(2):
            block = tok.at[(*own(k), slice(None), pl.ds(1024 * s, 1024))]
            for d in (1, -1, 2):
                net.start(("light", k, s), block, block, light(s, d))

    came = set()

    def tokens_heavy(q, s):
        if (q // 2, s) not in came:
            came.add((q // 2, s))
            three = tok.at[pl.ds(0, 3), 0, 0, 0, :, pl.ds(0, 1024)]
            net.arrived(("light", q // 2, s), three, light(s, 1))
        line = line_of(tok, q, s, here[s][0])
        for d in (1, -1, 2):
            net.start(("heavy", q, s), line, line, heavy(s, d))

    def tokens_in(q):
        for s in range(2):
            net.arrived(("heavy", q, s), tok.at[pl.ds(0, 3), :, 0, 0, :, pl.ds(0, 1024)], heavy(s, 1))

    def multiply(k, j):
        for i, (first, _) in enumerate(PARTS):
            if SPLIT[k][j][0] <= first < SPLIT[k][j][1]:
                weight(i)

        @pl.loop(*SPLIT[k][j])
        def _(n):
            cols = pl.ds(pl.multiple_of(n * 256, 256), 256)
            value = jnp.dot(tok[k].reshape(128, 2048), wgu[:, cols], preferred_element_type=F32)
            part[k, :, :, cols] = value.reshape(2, 64, 256)

        net.start(("pair", k, j), part.at[k, 1 - core, :, columns(k, j)], pair.at[k, :, columns(k, j)], mate)

    def total(k, j, rows, *more):
        cols = columns(k, j)
        value = part[k, core, rows, cols] + pair[k, rows, cols]
        for ref in more:
            value = value + ref[k, rows, cols].astype(F32)
        return value

    held = {}

    def end(k, j):
        return 2 if MEET[k][j] else 3

    def line_copy(k, j, up):
        src = zs.at[k, :, columns(k, j)]
        if up:
            return net.copy(held["line", k, j], ("line", k, j), src, zr.at[k, :, columns(k, j)], ahead)
        return net.copy(held["line", k, j], ("line", k, j), src, src, behind)

    def pass_on(k, j, up, *more):
        @pl.loop(0, 4)
        def _(r):
            rows = pl.ds(pl.multiple_of(r * 16, 16), 16)
            zs[k, rows, columns(k, j)] = total(k, j, rows, *more).astype(BF16)

        line_copy(k, j, up).start()

    def hidden_copy(k, j, name):
        block = hid.at[k, core, :, units(k, j)]
        final = k in EARLY and j == len(SPLIT[k]) - 1
        arrival = ("share", k, final) if name == "share" else ("back", k, j)
        device = {"share": mate, "back": behind, "onward": ahead}[name]
        return net.copy(held[name, k, j], arrival, block, block, device)

    def hidden_out(k, j, *names):
        for name in names:
            hidden_copy(k, j, name).start()

    def activate(k, j, *more):
        @pl.loop(0, 4)
        def _(r):
            rows = pl.ds(pl.multiple_of(r * 16, 16), 16)
            value = total(k, j, rows, *more)
            for n in range(SPLIT[k][j][1] - SPLIT[k][j][0]):
                g, u = value[:, 256 * n : 256 * n + 128], value[:, 256 * n + 128 : 256 * n + 256]
                unit = 128 * (SPLIT[k][j][0] + n)
                hid[k, core, rows, unit : unit + 128] = (g / (1.0 + jnp.exp(-g)) * u).astype(BF16)

    def line(k, j, p):
        if p == 0:
            held["line", k, j] = net.take()
            net.arrived(("pair", k, j), pair.at[k, :, columns(k, j)], mate)
        if p == end(k, j):
            for name in ("back", "share") + (("onward",) if MEET[k][j] else ()):
                held[name, k, j] = net.take()

        def go():
            if p == 0:
                pass_on(k, j, True)
                return
            if p == end(k, j) and MEET[k][j]:
                net.arrived(("line", k, j), zr.at[pl.ds(0, 2), :, columns(k, j)], behind)
            else:
                net.arrived(("line", k, j), zr.at[k, :, columns(k, j)], behind)
            if p < end(k, j):
                pass_on(k, j, True, zr)
            elif MEET[k][j]:
                activate(k, j, zr, zs)
                hidden_out(k, j, "back", "onward", "share")
            else:
                activate(k, j, zr)
                hidden_out(k, j, "back", "share")

        pl.when(pos == p)(go)
        if p == 0 and MEET[k][j]:
            pl.when(pos == 3)(lambda: pass_on(k, j, False))
        if p == end(k, j) - 1:
            net.give(held["line", k, j], line_copy(k, j, True), pos != end(k, j))

    backs = {}

    def back(k, j, p):
        def go():
            net.arrived(("back", k, j), hid.at[k, core, :, units(k, j)], ahead if p < end(k, j) else behind)
            hidden_out(k, j, *(("back",) if p and p < end(k, j) else ()), "share")

        pl.when(pos == p)(go)
        backs[k, j] = backs.get((k, j), 0) + 1
        if backs[k, j] == 3:
            senders = (pos == 1) | (pos == 2) if MEET[k][j] else pos > 0
            net.give(held["back", k, j], hidden_copy(k, j, "back"), senders)
            net.give(held["share", k, j], hidden_copy(k, j, "share"))
            if MEET[k][j]:
                net.give(held["onward", k, j], hidden_copy(k, j, "onward"), pos == 2)

    def down_product(q, s, first, last, more):
        if s == 0:
            weight(len(PARTS))
            net.arrived(("share", q, more), hid.at[q, 1 - core, :, pl.ds(first, last - first)], mate)

        @pl.loop(4 * s, 4 * s + 4)
        def _(n):
            cols = pl.ds(pl.multiple_of(n * 256, 256), 256)
            value = jnp.dot(
                hid[q, :, :, first:last].reshape(128, last - first), wd[first:last, cols], preferred_element_type=F32
            ).reshape(2, 2, 2, 16, 256)
            mix[q, :, :, :, :, cols] = mix[q, :, :, :, :, cols] + value if more else value

    def begin(q, s):
        down_product(q, s, 0, 128 * SPLIT[q][-1][0], False)

    def project(q, s):
        early = q in EARLY
        down_product(q, s, 128 * SPLIT[q][-1][0] if early else 0, 896, early)
        a, b = here[s]
        for i, d in enumerate((1, -1, 2)):
            s1[q, s, i] = line_of(mix, q, s, (a + d + 4) % 4)[...].astype(BF16)
            net.start(("last", q, s), s1.at[q, s, i], r1.at[q, s, i], heavy(s, d))

    def scatter_light(k, s):
        a, b = here[s]
        for p in range(2):
            q = 2 * k + p
            net.arrived(("last", q, s), r1.at[q, s], heavy(s, 1))
            value = line_of(mix, q, s, a)[...]
            for i in range(3):
                value = value + r1[q, s, i].astype(F32)
            for i in range(2):
                t1[k, s, 2 * i + (p + a) % 2] = value[i]
                t1s[k, s, 2 * i + (p + a) % 2] = value[i].astype(BF16)
        for i, d in enumerate((1, -1, 2)):
            net.start(("second", k, s), t1s.at[k, s, (b + d + 4) % 4], r2.at[k, s, i], light(s, d))

    def scatter_across(k, s):
        a, b = here[s]
        net.arrived(("second", k, s), r2.at[k, s], light(s, 1))
        value = t1[k, s, b]
        for i in range(3):
            value = value + r2[k, s, i].astype(F32)
        h = HALF_OF[k]
        if k in OTHER:
            t2[h, s] = value.astype(BF16)
            net.start(("third", h, s), t2.at[h, s], z3.at[h, s], across)
        else:
            net.arrived(("third", h, s), z3.at[h, s], across)
            out[16 * h : 16 * h + 16, 1024 * s : 1024 * s + 1024] = (value + z3[h, s].astype(F32)).astype(BF16)

    STEPS = (
        tokens_out, tokens_light, tokens_heavy, None, tokens_in, multiply,
        line, back, project, None, scatter_light, scatter_across, begin,
    )
    for number, *args in ORDER:
        STEPS[number](*args)
    net.finish()


def on_device(tokens, gate_weight, up_weight, down_weight):
    hbm = pl.BlockSpec(memory_space=pl.ANY)
    n, g = CHUNKS, GROUPS
    return pl.pallas_call(
        kernel,
        out_shape=pltpu.VMEM((32, 2048), BF16),
        in_specs=[hbm] * 4,
        out_specs=pl.BlockSpec(memory_space=pltpu.VMEM),
        scratch_shapes=[
            pltpu.VMEM((n, 2, 2, 2, 16, 2048), BF16),
            pltpu.VMEM((2048, 1792), BF16),
            pltpu.VMEM((896, 2048), BF16),
            pltpu.VMEM((n, 2, 64, 1792), F32),
            pltpu.VMEM((n, 64, 1792), F32),
            pltpu.VMEM((n, 64, 1792), BF16),
            pltpu.VMEM((n, 64, 1792), BF16),
            pltpu.VMEM((n, 2, 64, 896), BF16),
            pltpu.VMEM((n, 2, 2, 2, 16, 2048), F32),
            pltpu.VMEM((n, 2, 3, 2, 16, 1024), BF16),
            pltpu.VMEM((n, 2, 3, 2, 16, 1024), BF16),
            pltpu.VMEM((g, 2, 4, 16, 1024), F32),
            pltpu.VMEM((g, 2, 4, 16, 1024), BF16),
            pltpu.VMEM((g, 2, 3, 16, 1024), BF16),
            pltpu.VMEM((2, 2, 16, 1024), BF16),
            pltpu.VMEM((2, 2, 16, 1024), BF16),
            pltpu.SemaphoreType.DMA((3 + len(PARTS),)),
            pltpu.SemaphoreType.DMA((POOL,)),
            pltpu.SemaphoreType.DMA((ARRIVALS,)),
        ],
        compiler_params=pltpu.CompilerParams(
            collective_id=0, has_side_effects=True, vmem_limit_bytes=60 * 2**20
        ),
        name="panel",
    )(tokens, gate_weight, up_weight, down_weight)


def solution(mesh):
    return jax.shard_map(
        on_device,
        mesh=mesh,
        in_specs=(P("dp", "tensor"), P("tensor", "dp"), P("tensor", "dp"), P("dp", "tensor")),
        out_specs=P("dp", "tensor"),
        check_vma=False,
    )
```
